256 devices in a mesh: enc: 16 (over y, x), dom: 16 (over z, core).
Axes of the slice: x: 4, y: 4, z: 8, core: 2. Of those that a mesh axis runs over, the one named last changes fastest.
Arguments:
- residual: bfloat16 [4096, 4, 8192], P('enc', None, 'dom'), may hold values from -6 to 6
- weights: int32 [16, 4096], P(None, 'enc'), may hold values from -1 to 1, as said below
- source_pos: int32 [4096], replicated, may hold values from 0 to 4194303, as said below
- receiver_pos: int32 [8192], P('dom'), may hold values from 0 to 4194303, as said below
- wavelet: float32 [4], replicated, may hold values from -4 to 4
- courant: float32 [256, 128, 128], P('dom'), may hold values from 0.05 to 0.2
- fwd_prev: float32 [16, 256, 128, 128], P('enc', 'dom'), may hold values from -6 to 6
- fwd_now: float32 [16, 256, 128, 128], P('enc', 'dom'), may hold values from -6 to 6
- adj_next: float32 [16, 256, 128, 128], P('enc', 'dom'), may hold values from -6 to 6
- adj_now: float32 [16, 256, 128, 128], P('enc', 'dom'), may hold values from -6 to 6
Outputs:
- gradient: float32 [256, 128, 128], P('dom', 'enc')
- fwd_last: float32 [16, 256, 128, 128], P('enc', 'dom')
- adj_first: float32 [16, 256, 128, 128], P('enc', 'dom')
The draws below stay inside these ranges and needn't reach their ends.
Inputs may be any that keep to these rules, and one draw needn't show every extreme that they name: `weights`: every entry is -1 or 1. `source_pos`: flat cell index over the whole grid. `receiver_pos`: receiver r lies in depth slab r // 512: its flat index lies in [(r // 512) * 16 * 128 * 128, (r // 512 + 1) * 16 * 128 * 128).
All inputs are finite; a program needn't handle non-finite values.
Results may differ from the reference program's by a relative error of at most 0.0003.
Values may be sent and summed in bfloat16 or wider, within the bound.
A program may use at most 128 MiB of HBM per device.

```python
import math
import jax
import jax.numpy as jnp
from jax import lax

CZ = 16
NX = 128
NY = 128
STEPS = 4
RECV_DEV = 512
NZ = 256
SHOTS = 4096
SUPERSHOTS = 16
RECV = 8192


def draw_weights(key, part):
    key = jax.random.fold_in(key, 11)
    return 2 * jax.random.randint(key, (SUPERSHOTS, SHOTS), 0, 2, dtype=jnp.int32) - 1


def draw_source_pos(key, part):
    key = jax.random.fold_in(key, 23)
    total = NZ * NX * NY
    picks = jax.random.randint(key, (SHOTS,), 0, total, dtype=jnp.int32)
    picks = picks.at[0].set(0)
    return picks.at[SHOTS - 1].set(total - 1)


def draw_receiver_pos(key, part):
    key = jax.random.fold_in(key, 37)
    slab = CZ * NX * NY
    offset = jax.random.randint(key, (RECV,), 0, slab, dtype=jnp.int32)
    offset = offset.at[0].set(0)
    offset = offset.at[RECV - 1].set(slab - 1)
    block = jnp.arange(RECV, dtype=jnp.int32) // RECV_DEV
    return block * slab + offset


def steps_of(rng, extent, cuts, low, high):
    loudness, own = 1.0, jax.random.fold_in(rng, 6)
    for axis_at, shards_of in cuts:
        steps = jnp.exp(jax.random.uniform(jax.random.fold_in(own, axis_at), (shards_of,), jnp.float32, low / len(cuts), high / len(cuts)))
        loudness = loudness * jnp.repeat(steps, extent[axis_at] // shards_of).reshape([-1 if axis == axis_at else 1 for axis in range(len(extent))])
    return loudness


def scatter_about(stream_key, shape, deviation, reach, cuts=(), kind=jnp.bfloat16):
    result = deviation * jax.random.normal(stream_key, shape, jnp.float32)
    if cuts:
        result = result * steps_of(stream_key, shape, cuts, -0.22, 0.18)
    return jnp.clip(result, -reach, reach).astype(kind)


def setup_inputs(seed: int = 0) -> dict:
    seeds = jax.random.split(jax.random.key(seed), 11)
    return {
        "residual": scatter_about(seeds[0], (SHOTS, STEPS, RECV), 1.0, 6.0, ((0, 16), (2, 16))),
        "weights": draw_weights(jax.random.fold_in(seeds[10], 71), 0),
        "source_pos": draw_source_pos(jax.random.fold_in(seeds[10], 71), 0),
        "receiver_pos": draw_receiver_pos(jax.random.fold_in(seeds[10], 71), 0),
        "wavelet": scatter_about(seeds[4], (STEPS,), 1.0, 4.0, (), jnp.float32),
        "courant": jnp.clip(jnp.exp(math.log(0.2) - 1.3862944 * jax.random.uniform(seeds[5], (NZ, NX, NY), jnp.float32) ** steps_of(seeds[5], (NZ, NX, NY), ((0, 16),), -0.2, 0.2)), 0.05, 0.2),
        "fwd_prev": scatter_about(seeds[6], (SUPERSHOTS, NZ, NX, NY), 1.0, 6.0, ((0, 16), (1, 16)), jnp.float32),
        "fwd_now": scatter_about(seeds[7], (SUPERSHOTS, NZ, NX, NY), 1.0, 6.0, ((0, 16), (1, 16)), jnp.float32),
        "adj_next": scatter_about(seeds[8], (SUPERSHOTS, NZ, NX, NY), 1.0, 6.0, ((0, 16), (1, 16)), jnp.float32),
        "adj_now": scatter_about(seeds[9], (SUPERSHOTS, NZ, NX, NY), 1.0, 6.0, ((0, 16), (1, 16)), jnp.float32),
    }


center_coeff = -205.0 / 72.0
cycle_coeffs = (1.6, -0.2, 8.0 / 315.0, -1.0 / 560.0)

def apply_stencil(padded):
    depth = padded.shape[0] - 8
    width = padded.shape[1] - 8
    length = padded.shape[2] - 8
    inner = padded[4:4 + depth, 4:4 + width, 4:4 + length]
    total = 3.0 * center_coeff * inner
    for k in range(4):
        off = k + 1
        near = padded[4 + off:4 + off + depth, 4:4 + width, 4:4 + length] + padded[4 - off:4 - off + depth, 4:4 + width, 4:4 + length]
        near = near + padded[4:4 + depth, 4 + off:4 + off + width, 4:4 + length] + padded[4:4 + depth, 4 - off:4 - off + width, 4:4 + length]
        near = near + padded[4:4 + depth, 4:4 + width, 4 + off:4 + off + length] + padded[4:4 + depth, 4:4 + width, 4 - off:4 - off + length]
        total = total + cycle_coeffs[k] * near
    return total

def laplace(field):
    return apply_stencil(jnp.pad(field, 4))

def reference(residual, weights, source_pos, receiver_pos, wavelet, courant, fwd_prev, fwd_now, adj_next, adj_now):
    flat = residual.reshape(SHOTS, STEPS * RECV)
    encoded = jnp.dot(weights.astype(jnp.bfloat16), flat, preferred_element_type=jnp.float32) * (1.0 / math.sqrt(SHOTS))
    encoded = encoded.reshape(SUPERSHOTS, STEPS, RECV)
    cells = NZ * NX * NY

    def one_shot(items):
        row, enc_rows, prev_f, now_f, later_a, now_a = items
        pattern = jnp.zeros((cells,), jnp.float32).at[source_pos].add(row.astype(jnp.float32)).reshape(NZ, NX, NY)
        images = []
        for t in range(STEPS):
            image = laplace(now_f)
            images.append(image)
            nxt = 2.0 * now_f - prev_f + courant * image + wavelet[t] * pattern
            prev_f, now_f = (now_f, nxt)
        grad = jnp.zeros((NZ, NX, NY), jnp.float32)
        for k in range(STEPS):
            t = STEPS - 1 - k
            inject = jnp.zeros((cells,), jnp.float32).at[receiver_pos].add(enc_rows[t]).reshape(NZ, NX, NY)
            new = 2.0 * now_a - later_a + laplace(courant * now_a) + inject
            grad = grad + new * images[t]
            later_a, now_a = (now_a, new)
        return (grad, now_f, now_a)
    grads, fwd_last, adj_first = lax.map(one_shot, (weights, encoded, fwd_prev, fwd_now, adj_next, adj_now))
    gradient = lax.optimization_barrier(jnp.sum(grads, axis=0)) * (1.0 / (STEPS * SUPERSHOTS))
    return (gradient, fwd_last, adj_first)
```

```python
import functools

import jax
import jax.numpy as jnp
from jax import lax
from jax.experimental import pallas as pl
from jax.experimental.pallas import tpu as pltpu
from jax.sharding import PartitionSpec as P

MESH = pl.DeviceIdType.MESH
F32 = jnp.float32
BF16 = jnp.bfloat16
UNIT = 5040.0
CENTER = 3.0 * -14350.0
RINGS = (8064.0, -1008.0, 128.0, -9.0)
PAD = 8
HALO = 4


def kernel(
    n,
    nd,
    residual,
    weights,
    source_pos,
    receiver_pos,
    wavelet,
    courant,
    fwd_prev,
    fwd_now,
    adj_next,
    adj_now,
    gradient,
    fwd_last,
    adj_first,
    res_v,
    cour_v,
    u_a,
    u_b,
    w_a,
    w_b,
    a_4,
    a_5,
    a_1,
    image_0,
    image_1,
    grad,
    pattern,
    inject,
    band,
    rows_hot,
    cols_hot,
    part,
    parts,
    gsend,
    grecv,
    gout,
    load_sem,
    store_sem,
    enc_send,
    enc_recv,
    halo_send,
    halo_recv,
    grad_send,
    grad_recv,
):
    depth, width, length = cour_v.shape
    shots = weights.shape[1]
    steps = res_v.shape[1]
    recvs = receiver_pos.shape[1]
    shift = width.bit_length() - 1
    e = lax.axis_index("enc")
    d = lax.axis_index("dom")
    inner = pl.ds(HALO, depth)
    body_rows = pl.ds(PAD, width)

    loads = [
        pltpu.make_async_copy(fwd_now.at[0], u_a.at[inner, body_rows, :], load_sem.at[0]),
        pltpu.make_async_copy(adj_now.at[0], a_4, load_sem.at[1]),
        pltpu.make_async_copy(courant, cour_v, load_sem.at[2]),
        pltpu.make_async_copy(residual, res_v, load_sem.at[3]),
        pltpu.make_async_copy(fwd_prev.at[0], u_b.at[inner, body_rows, :], load_sem.at[4]),
        pltpu.make_async_copy(adj_next.at[0], a_5, load_sem.at[5]),
    ]
    for copy in loads:
        copy.start()

    for field in (u_a, u_b, w_a, w_b):
        edge = jnp.zeros((depth + 2 * HALO, PAD, length), F32)
        field[:, pl.ds(0, PAD), :] = edge
        field[:, pl.ds(PAD + width, PAD), :] = edge

        @pl.when(d == 0)
        def _():
            field[pl.ds(0, HALO)] = jnp.zeros((HALO, width + 2 * PAD, length), F32)

        @pl.when(d == nd - 1)
        def _():
            field[pl.ds(HALO + depth, HALO)] = jnp.zeros((HALO, width + 2 * PAD, length), F32)

    barrier = pltpu.get_barrier_semaphore()

    def greet(k, carry):
        pl.semaphore_signal(
            barrier, inc=1, device_id={"enc": lax.rem(e + k, n)}, device_id_type=MESH
        )
        return carry

    lax.fori_loop(1, n, greet, 0)

    @pl.when(d > 0)
    def _():
        pl.semaphore_signal(barrier, inc=1, device_id={"dom": d - 1}, device_id_type=MESH)

    @pl.when(d < nd - 1)
    def _():
        pl.semaphore_signal(barrier, inc=1, device_id={"dom": d + 1}, device_id_type=MESH)

    pl.semaphore_wait(
        barrier, n - 1 + (d > 0).astype(jnp.int32) + (d < nd - 1).astype(jnp.int32)
    )

    def halo_copy(h, source, field, down):
        near = 0 if down else depth - HALO
        if source is field:
            src = field.at[pl.ds(HALO + near, HALO), body_rows, :]
        else:
            src = source.at[0, pl.ds(near, HALO)]
        far = HALO + depth if down else 0
        way = 0 if down else 1
        return pltpu.make_async_remote_copy(
            src_ref=src,
            dst_ref=field.at[pl.ds(far, HALO), body_rows, :],
            send_sem=halo_send.at[h, way],
            recv_sem=halo_recv.at[h, way],
            device_id={"dom": d - 1 if down else d + 1},
            device_id_type=MESH,
        )

    def halo_start(h, source, field):
        @pl.when(d > 0)
        def _():
            halo_copy(h, source, field, True).start()

        @pl.when(d < nd - 1)
        def _():
            halo_copy(h, source, field, False).start()

    def halo_sent(h, source, field):
        @pl.when(d > 0)
        def _():
            halo_copy(h, source, field, True).wait_send()

        @pl.when(d < nd - 1)
        def _():
            halo_copy(h, source, field, False).wait_send()

    def halo_wait(h, source, field):
        @pl.when(d < nd - 1)
        def _():
            halo_copy(h, source, field, True).wait_recv()

        @pl.when(d > 0)
        def _():
            halo_copy(h, source, field, False).wait_recv()

    halo_start(0, fwd_now, u_a)

    loads[1].wait()
    loads[2].wait()

    def scale_tile(j, carry):
        rows = pl.ds(pl.multiple_of(j * 8, 8), 8)
        scaled = cour_v[:, rows, :] * (1.0 / UNIT)
        cour_v[:, rows, :] = scaled
        w_a[inner, pl.ds(pl.multiple_of(j * 8 + PAD, 8), 8), :] = scaled * a_4[:, rows, :]
        return carry

    lax.fori_loop(0, width // 8, scale_tile, 0)
    halo_start(1, w_a, w_a)

    signs = weights[...].astype(F32)
    shot_of = lax.shift_right_logical(lax.broadcasted_iota(jnp.int32, (shots, shots * steps), 1), 2)
    spread = jnp.where(
        shot_of == lax.broadcasted_iota(jnp.int32, (shots, shots * steps), 0), 1.0, 0.0
    ).astype(BF16)
    wide = jnp.dot(signs.astype(BF16), spread, preferred_element_type=F32)
    wide = jnp.broadcast_to(wide[:, None, :], (n, 8, shots * steps))
    same_step = (
        lax.broadcasted_iota(jnp.int32, (n, 8, shots * steps), 2) & (steps - 1)
    ) == lax.broadcasted_iota(jnp.int32, (n, 8, shots * steps), 1)
    wide = jnp.where(same_step, wide, 0.0).reshape(n * 8, shots * steps).astype(BF16)
    loads[3].wait()
    traces = jnp.dot(
        wide, res_v[...].reshape(shots * steps, recvs), preferred_element_type=F32
    )
    part[...] = traces.reshape(n, 8, recvs)
    part[:, steps, pl.ds(0, shots)] = signs
    parts[e] = part[e]

    def enc_copy(k, incoming):
        to = lax.rem(e + k, n)
        slot = lax.rem(e - k + n, n) if incoming else e
        return pltpu.make_async_remote_copy(
            src_ref=part.at[to],
            dst_ref=parts.at[slot],
            send_sem=enc_send.at[k],
            recv_sem=enc_recv.at[k],
            device_id={"enc": to},
            device_id_type=MESH,
        )

    def enc_start(k, carry):
        enc_copy(k, False).start()
        return carry

    lax.fori_loop(1, n, enc_start, 0)

    across = lax.broadcasted_iota(jnp.int32, (2 * length, length), 0) & (length - 1)
    gap = jnp.abs(across - lax.broadcasted_iota(jnp.int32, (2 * length, length), 1))
    weight = jnp.zeros((2 * length, length), F32)
    for k in range(4):
        weight = jnp.where(gap == k + 1, RINGS[k], weight)
    band[...] = weight.astype(BF16)

    base = d * (depth * width * length)
    hot_rows = 4 * width
    hot_cols = 4 * length

    def row_of(cell):
        return (lax.shift_right_arithmetic(cell, shift + 9) << shift) | (
            lax.shift_right_arithmetic(cell, 7) & (width - 1)
        )

    def col_of(cell):
        return ((lax.shift_right_arithmetic(cell, shift + 7) & 3) << 7) | (cell & 127)

    def enc_wait(k, carry):
        enc_copy(k, True).wait_recv()
        return carry

    lax.fori_loop(1, n, enc_wait, 0)

    total = parts[0]
    for i in range(1, n):
        total = total + parts[i]
    total = total * (1.0 / (shots * n) ** 0.5)
    cell = receiver_pos[...] - base
    row_hot = jnp.where(
        lax.broadcasted_iota(jnp.int32, (hot_rows, recvs), 0) == row_of(cell), 1.0, 0.0
    ).astype(BF16)
    rows_hot[:, pl.ds(0, recvs)] = row_hot
    rows_hot[:, pl.ds(recvs, recvs)] = row_hot
    col_hit = lax.broadcasted_iota(jnp.int32, (hot_cols, recvs), 0) == col_of(cell)
    for t in range(steps):
        value = total[t : t + 1, :]
        high = value.astype(BF16).astype(F32)
        cols_hot[:, pl.ds(0, recvs)] = jnp.where(col_hit, high, 0.0).astype(BF16)
        cols_hot[:, pl.ds(recvs, recvs)] = jnp.where(col_hit, value - high, 0.0).astype(BF16)

        def receivers(q, carry):
            placed = lax.dot_general(
                rows_hot[pl.ds(pl.multiple_of(q * width, width), width), pl.ds(0, 2 * recvs)],
                cols_hot[:, pl.ds(0, 2 * recvs)],
                (((1,), (1,)), ((), ())),
                preferred_element_type=F32,
            )
            for r in range(4):
                inject[t, q * 4 + r] = placed[:, r * length : (r + 1) * length]
            return carry

        lax.fori_loop(0, 4, receivers, 0)

    group = 4

    def sources(g, carry):
        for i in range(group):
            at = g * group + i
            cell = source_pos[at] - base
            cols = pl.ds(i * shots, shots)
            rows_hot[:, cols] = jnp.where(
                lax.broadcasted_iota(jnp.int32, (hot_rows, shots), 0) == row_of(cell), 1.0, 0.0
            ).astype(BF16)
            sign = parts[at, steps : steps + 1, pl.ds(0, shots)]
            cols_hot[:, cols] = jnp.where(
                lax.broadcasted_iota(jnp.int32, (hot_cols, shots), 0) == col_of(cell), sign, 0.0
            ).astype(BF16)
        for q in range(4):
            placed = lax.dot_general(
                rows_hot[pl.ds(q * width, width), pl.ds(0, group * shots)],
                cols_hot[:, pl.ds(0, group * shots)],
                (((1,), (1,)), ((), ())),
                preferred_element_type=F32,
            )
            for r in range(4):
                pattern[q * 4 + r] += placed[:, r * length : (r + 1) * length]
        return carry

    pattern[...] = jnp.zeros(pattern.shape, F32)
    lax.fori_loop(0, n // group, sources, 0)

    def laplace(field, x0):
        column = field[:, pl.ds(pl.multiple_of(x0 + PAD, 8), 8), :]
        mid = column[HALO : HALO + depth]
        flat = mid.reshape(depth * 8, length)
        high = flat.astype(BF16)
        low = (flat - high.astype(F32)).astype(BF16)
        lanes = jnp.dot(
            jnp.concatenate([high, low], axis=1), band[...], preferred_element_type=F32
        ).reshape(depth, 8, length)
        total = CENTER * mid + lanes
        for k in range(4):
            near = column[HALO + 1 + k : HALO + 1 + k + depth] + column[3 - k : 3 - k + depth]
            near = near + field[inner, pl.ds(x0 + PAD + 1 + k, 8), :]
            near = near + field[inner, pl.ds(x0 + PAD - 1 - k, 8), :]
            total = total + RINGS[k] * near
        return mid, total

    def forward(t, now, prev):
        def tile(j, carry):
            x0 = pl.multiple_of(j * 8, 8)
            rows = pl.ds(x0, 8)
            padded = pl.ds(pl.multiple_of(x0 + PAD, 8), 8)
            mid, image = laplace(now, x0)
            prev[inner, padded, :] = (
                (mid + mid - prev[inner, padded, :])
                + cour_v[:, rows, :] * image
                + wavelet[t] * pattern[:, rows, :]
            )
            if t == 0:
                image_0[:, rows, :] = image
            elif t == 1:
                image_1[:, rows, :] = image
            elif t == 2:
                grad[:, rows, :] = image * a_4[:, rows, :]
            else:
                grad[:, rows, :] += image * a_5[:, rows, :]
            return carry

        lax.fori_loop(0, width // 8, tile, 0)

    def grad_copy(to, slot):
        return pltpu.make_async_remote_copy(
            src_ref=gsend.at[to],
            dst_ref=grecv.at[slot],
            send_sem=grad_send.at[to],
            recv_sem=grad_recv.at[slot],
            device_id={"enc": to},
            device_id_type=MESH,
        )

    def adjoint(t, w_now, w_next, now, later, new):
        def tile(i, carry):
            j = lax.rem(e + 1 + i, n) if t == 0 else i
            x0 = pl.multiple_of(j * 8, 8)
            rows = pl.ds(x0, 8)
            _, along = laplace(w_now, x0)
            value = now[:, rows, :]
            value = (value + value - later[:, rows, :]) + along + inject[t, :, rows, :]
            new[:, rows, :] = value
            if t > 0:
                w_next[inner, pl.ds(pl.multiple_of(x0 + PAD, 8), 8), :] = cour_v[:, rows, :] * value
            if t == 1:
                grad[:, rows, :] += value * image_1[:, rows, :]
            if t == 0:
                gsend[j] = grad[:, rows, :] + value * image_0[:, rows, :]

                @pl.when(j != e)
                def _():
                    grad_copy(j, e).start()

            return carry

        lax.fori_loop(0, width // 8, tile, 0)

    loads[0].wait()
    loads[4].wait()
    loads[5].wait()
    halo_wait(0, fwd_now, u_a)
    forward(0, u_a, u_b)
    halo_start(2, u_b, u_b)
    halo_wait(1, w_a, w_a)
    adjoint(3, w_a, w_b, a_4, a_5, a_5)
    halo_start(3, w_b, w_b)

    halo_wait(2, u_b, u_b)
    halo_sent(0, fwd_now, u_a)
    forward(1, u_b, u_a)
    halo_start(4, u_a, u_a)
    halo_wait(3, w_b, w_b)
    halo_sent(1, w_a, w_a)
    adjoint(2, w_b, w_a, a_5, a_4, a_4)
    halo_start(5, w_a, w_a)

    halo_wait(4, u_a, u_a)
    halo_sent(2, u_b, u_b)
    forward(2, u_a, u_b)
    halo_start(6, u_b, u_b)
    halo_wait(5, w_a, w_a)
    halo_sent(3, w_b, w_b)
    adjoint(1, w_a, w_b, a_4, a_5, a_1)
    halo_start(7, w_b, w_b)

    halo_wait(6, u_b, u_b)
    halo_sent(4, u_a, u_a)
    forward(3, u_b, u_a)
    store_u = pltpu.make_async_copy(u_a.at[inner, body_rows, :], fwd_last.at[0], store_sem.at[0])
    store_u.start()
    halo_wait(7, w_b, w_b)
    adjoint(0, w_b, None, a_1, a_4, a_4)
    store_a = pltpu.make_async_copy(a_4, adj_first.at[0], store_sem.at[1])
    store_a.start()

    def grad_wait(k, share):
        slot = lax.rem(e + k, n)
        grad_copy(slot, slot).wait_recv()
        return share + grecv[slot]

    share = lax.fori_loop(1, n, grad_wait, gsend[e])
    gout[...] = share * (1.0 / (UNIT * steps * n))
    store_g = pltpu.make_async_copy(gout, gradient, store_sem.at[2])
    store_g.start()

    def finish(k, carry):
        enc_copy(k, False).wait_send()
        to = lax.rem(e + k, n)
        grad_copy(to, to).wait_send()
        return carry

    lax.fori_loop(1, n, finish, 0)
    halo_sent(5, w_a, w_a)
    halo_sent(6, u_b, u_b)
    halo_sent(7, w_b, w_b)
    store_u.wait()
    store_a.wait()
    store_g.wait()


def body(
    n,
    nd,
    residual,
    weights,
    source_pos,
    receiver_pos,
    wavelet,
    courant,
    fwd_prev,
    fwd_now,
    adj_next,
    adj_now,
):
    shots, steps, recvs = residual.shape
    depth, width, length = courant.shape
    share = (depth, width // n, length)
    field = pltpu.VMEM((depth, width, length), F32)
    padded = pltpu.VMEM((depth + 2 * HALO, width + 2 * PAD, length), F32)
    hot = max(2 * recvs, 4 * shots)
    anywhere = pl.BlockSpec(memory_space=pl.ANY)
    vmem = pl.BlockSpec(memory_space=pltpu.VMEM)
    return pl.pallas_call(
        functools.partial(kernel, n, nd),
        out_shape=(
            jax.ShapeDtypeStruct(share, F32),
            jax.ShapeDtypeStruct((1, depth, width, length), F32),
            jax.ShapeDtypeStruct((1, depth, width, length), F32),
        ),
        in_specs=[
            anywhere,
            vmem,
            vmem,
            vmem,
            pl.BlockSpec(memory_space=pltpu.SMEM),
            anywhere,
            anywhere,
            anywhere,
            anywhere,
            anywhere,
        ],
        out_specs=(anywhere, anywhere, anywhere),
        scratch_shapes=[
            pltpu.VMEM((shots, steps, recvs), BF16),
            field,
            padded,
            padded,
            padded,
            padded,
            field,
            field,
            field,
            field,
            field,
            field,
            field,
            pltpu.VMEM((steps, depth, width, length), F32),
            pltpu.VMEM((2 * length, length), BF16),
            pltpu.VMEM((4 * width, hot), BF16),
            pltpu.VMEM((4 * length, hot), BF16),
            pltpu.VMEM((n, 8, recvs), F32),
            pltpu.VMEM((n, 8, recvs), F32),
            pltpu.VMEM((n,) + share, F32),
            pltpu.VMEM((n,) + share, F32),
            pltpu.VMEM(share, F32),
            pltpu.SemaphoreType.DMA((6,)),
            pltpu.SemaphoreType.DMA((3,)),
            pltpu.SemaphoreType.DMA((n,)),
            pltpu.SemaphoreType.DMA((n,)),
            pltpu.SemaphoreType.DMA((8, 2)),
            pltpu.SemaphoreType.DMA((8, 2)),
            pltpu.SemaphoreType.DMA((n,)),
            pltpu.SemaphoreType.DMA((n,)),
        ],
        compiler_params=pltpu.CompilerParams(
            collective_id=0, has_side_effects=True, vmem_limit_bytes=56 * 2**20
        ),
    )(
        residual,
        weights,
        source_pos.reshape(n, 1, shots),
        receiver_pos.reshape(1, recvs),
        wavelet,
        courant,
        fwd_prev,
        fwd_now,
        adj_next,
        adj_now,
    )


def solution(mesh):
    placed = (
        P("enc", None, "dom"),
        P(None, "enc"),
        P(),
        P("dom"),
        P(),
        P("dom", None, None),
        P("enc", "dom", None, None),
        P("enc", "dom", None, None),
        P("enc", "dom", None, None),
        P("enc", "dom", None, None),
    )
    return jax.shard_map(
        functools.partial(body, mesh.shape["enc"], mesh.shape["dom"]),
        mesh=mesh,
        in_specs=placed,
        out_specs=(P("dom", "enc", None), P("enc", "dom", None, None), P("enc", "dom", None, None)),
        check_vma=False,
    )
```

```python
import functools

import jax
import jax.numpy as jnp
from jax import lax
from jax.experimental import pallas as pl
from jax.experimental.pallas import tpu as pltpu
from jax.sharding import PartitionSpec as P

MESH = pl.DeviceIdType.MESH
F32 = jnp.float32
BF16 = jnp.bfloat16
UNIT = 5040.0
CENTER = 3.0 * -14350.0
RINGS = (8064.0, -1008.0, 128.0, -9.0)
PAD = 8
HALO = 4
TILE = 16
UNROLL = 4
LAST_UNROLL = 4


def kernel(
    n,
    nd,
    residual,
    weights,
    source_pos,
    receiver_pos,
    wavelet,
    courant,
    fwd_prev,
    fwd_now,
    adj_next,
    adj_now,
    gradient,
    fwd_last,
    adj_first,
    res_v,
    cour_v,
    u_a,
    u_b,
    w_a,
    w_b,
    a_4,
    a_5,
    a_1,
    image_0,
    image_1,
    grad,
    pattern,
    inject,
    band,
    src_rows,
    recv_rows,
    cols_hot,
    part,
    parts,
    traces_v,
    gsend,
    grecv,
    gout,
    load_sem,
    store_sem,
    enc_send,
    enc_recv,
    halo_send,
    halo_recv,
    grad_send,
    grad_recv,
):
    depth, width, length = cour_v.shape
    shots = weights.shape[1]
    steps = res_v.shape[1]
    recvs = receiver_pos.shape[1]
    shift = width.bit_length() - 1
    e = lax.axis_index("enc")
    d = lax.axis_index("dom")
    inner = pl.ds(HALO, depth)
    body_rows = pl.ds(PAD, width)

    loads = [
        pltpu.make_async_copy(fwd_now.at[0], u_a.at[inner, body_rows, :], load_sem.at[0]),
        pltpu.make_async_copy(adj_now.at[0], a_4, load_sem.at[1]),
        pltpu.make_async_copy(courant, cour_v, load_sem.at[2]),
        pltpu.make_async_copy(residual, res_v, load_sem.at[3]),
        pltpu.make_async_copy(fwd_prev.at[0], u_b.at[inner, body_rows, :], load_sem.at[4]),
        pltpu.make_async_copy(adj_next.at[0], a_5, load_sem.at[5]),
    ]
    for copy in loads:
        copy.start()

    barrier = pltpu.get_barrier_semaphore()

    def greet(k, carry):
        pl.semaphore_signal(
            barrier, inc=1, device_id={"enc": lax.rem(e + k, n)}, device_id_type=MESH
        )
        return carry

    lax.fori_loop(1, n, greet, 0)

    @pl.when(d > 0)
    def _():
        pl.semaphore_signal(barrier, inc=1, device_id={"dom": d - 1}, device_id_type=MESH)

    @pl.when(d < nd - 1)
    def _():
        pl.semaphore_signal(barrier, inc=1, device_id={"dom": d + 1}, device_id_type=MESH)

    for field in (u_a, u_b, w_a, w_b):
        edge = jnp.zeros((depth + 2 * HALO, PAD, length), F32)
        field[:, pl.ds(0, PAD), :] = edge
        field[:, pl.ds(PAD + width, PAD), :] = edge

        @pl.when(d == 0)
        def _():
            field[pl.ds(0, HALO)] = jnp.zeros((HALO, width + 2 * PAD, length), F32)

        @pl.when(d == nd - 1)
        def _():
            field[pl.ds(HALO + depth, HALO)] = jnp.zeros((HALO, width + 2 * PAD, length), F32)

    loads[1].wait()
    loads[2].wait()

    def scale_tile(j, carry):
        rows = pl.ds(pl.multiple_of(j * 8, 8), 8)
        scaled = cour_v[:, rows, :] * (1.0 / UNIT)
        cour_v[:, rows, :] = scaled
        w_a[inner, pl.ds(pl.multiple_of(j * 8 + PAD, 8), 8), :] = scaled * a_4[:, rows, :]
        return carry

    lax.fori_loop(0, width // 8, scale_tile, 0)

    pl.semaphore_wait(
        barrier, n - 1 + (d > 0).astype(jnp.int32) + (d < nd - 1).astype(jnp.int32)
    )

    def halo_copy(h, source, field, down):
        near = 0 if down else depth - HALO
        if source is field:
            src = field.at[pl.ds(HALO + near, HALO), body_rows, :]
        else:
            src = source.at[0, pl.ds(near, HALO)]
        far = HALO + depth if down else 0
        way = 0 if down else 1
        return pltpu.make_async_remote_copy(
            src_ref=src,
            dst_ref=field.at[pl.ds(far, HALO), body_rows, :],
            send_sem=halo_send.at[h, way],
            recv_sem=halo_recv.at[h, way],
            device_id={"dom": d - 1 if down else d + 1},
            device_id_type=MESH,
        )

    def halo_start(h, source, field):
        @pl.when(d > 0)
        def _():
            halo_copy(h, source, field, True).start()

        @pl.when(d < nd - 1)
        def _():
            halo_copy(h, source, field, False).start()

    def halo_sent(h, source, field):
        @pl.when(d > 0)
        def _():
            halo_copy(h, source, field, True).wait_send()

        @pl.when(d < nd - 1)
        def _():
            halo_copy(h, source, field, False).wait_send()

    def halo_wait(h, source, field):
        @pl.when(d < nd - 1)
        def _():
            halo_copy(h, source, field, True).wait_recv()

        @pl.when(d > 0)
        def _():
            halo_copy(h, source, field, False).wait_recv()

    halo_start(0, fwd_now, u_a)
    halo_start(1, w_a, w_a)

    signs = weights[...].astype(F32)
    shot_of = lax.shift_right_logical(lax.broadcasted_iota(jnp.int32, (shots, shots * steps), 1), 2)
    spread = jnp.where(
        shot_of == lax.broadcasted_iota(jnp.int32, (shots, shots * steps), 0), 1.0, 0.0
    ).astype(BF16)
    wide = jnp.dot(signs.astype(BF16), spread, preferred_element_type=F32)
    wide = jnp.broadcast_to(wide[:, None, :], (n, 8, shots * steps))
    same_step = (
        lax.broadcasted_iota(jnp.int32, (n, 8, shots * steps), 2) & (steps - 1)
    ) == lax.broadcasted_iota(jnp.int32, (n, 8, shots * steps), 1)
    wide = jnp.where(same_step, wide, 0.0).reshape(n * 8, shots * steps).astype(BF16)
    loads[3].wait()
    traces = jnp.dot(
        wide, res_v[...].reshape(shots * steps, recvs), preferred_element_type=F32
    )
    part[...] = traces.reshape(n, 8, recvs)
    part[:, steps, pl.ds(0, shots)] = signs
    parts[e] = part[e]

    def enc_copy(k, incoming):
        to = lax.rem(e + k, n)
        slot = lax.rem(e - k + n, n) if incoming else e
        return pltpu.make_async_remote_copy(
            src_ref=part.at[to],
            dst_ref=parts.at[slot],
            send_sem=enc_send.at[k],
            recv_sem=enc_recv.at[k],
            device_id={"enc": to},
            device_id_type=MESH,
        )

    def enc_start(k, carry):
        enc_copy(k, False).start()
        return carry

    lax.fori_loop(1, n, enc_start, 0)

    across = lax.broadcasted_iota(jnp.int32, (2 * length, length), 0) & (length - 1)
    gap = jnp.abs(across - lax.broadcasted_iota(jnp.int32, (2 * length, length), 1))
    weight = jnp.zeros((2 * length, length), F32)
    for k in range(4):
        weight = jnp.where(gap == k + 1, RINGS[k], weight)
    band[...] = weight.astype(BF16)

    base = d * (depth * width * length)
    hot_rows = 4 * width
    hot_cols = 4 * length

    def row_of(cell):
        return (lax.shift_right_arithmetic(cell, shift + 9) << shift) | (
            lax.shift_right_arithmetic(cell, 7) & (width - 1)
        )

    def col_of(cell):
        return ((lax.shift_right_arithmetic(cell, shift + 7) & 3) << 7) | (cell & 127)

    def enc_wait(k, carry):
        enc_copy(k, True).wait_recv()
        return carry

    group = 4

    def source_rows(g, carry):
        for i in range(group):
            cell = source_pos[g * group + i] - base
            src_rows[g, :, pl.ds(i * shots, shots)] = jnp.where(
                lax.broadcasted_iota(jnp.int32, (hot_rows, shots), 0) == row_of(cell), 1.0, 0.0
            ).astype(BF16)
        return carry

    lax.fori_loop(0, n // group, source_rows, 0)
    recv_cell = receiver_pos[...] - base
    row_hot = jnp.where(
        lax.broadcasted_iota(jnp.int32, (hot_rows, recvs), 0) == row_of(recv_cell), 1.0, 0.0
    ).astype(BF16)
    recv_rows[:, pl.ds(0, recvs)] = row_hot
    recv_rows[:, pl.ds(recvs, recvs)] = row_hot

    def spread_out(rows, cols):
        return lax.dot_general(
            rows, cols, (((1,), (1,)), ((), ())), preferred_element_type=F32
        )

    def sources(g, carry):
        for i in range(group):
            at = g * group + i
            cell = source_pos[at] - base
            sign = parts[at, steps : steps + 1, pl.ds(0, shots)]
            cols_hot[:, pl.ds(i * shots, shots)] = jnp.where(
                lax.broadcasted_iota(jnp.int32, (hot_cols, shots), 0) == col_of(cell), sign, 0.0
            ).astype(BF16)
        placed = spread_out(src_rows[g], cols_hot[:, pl.ds(0, group * shots)])
        for q in range(4):
            for r in range(4):
                pattern[q * 4 + r] += placed[
                    q * width : (q + 1) * width, r * length : (r + 1) * length
                ]
        return carry

    def receivers(t):
        value = traces_v[t : t + 1, :]
        high = value.astype(BF16).astype(F32)
        hit = lax.broadcasted_iota(jnp.int32, (hot_cols, recvs), 0) == col_of(recv_cell)
        cols_hot[:, pl.ds(0, recvs)] = jnp.where(hit, high, 0.0).astype(BF16)
        cols_hot[:, pl.ds(recvs, recvs)] = jnp.where(hit, value - high, 0.0).astype(BF16)
        placed = spread_out(recv_rows[...], cols_hot[:, pl.ds(0, 2 * recvs)])
        for q in range(4):
            for r in range(4):
                inject[t, q * 4 + r] = placed[
                    q * width : (q + 1) * width, r * length : (r + 1) * length
                ]

    def laplace(field, z0, nz, x0, nx):
        column = field[pl.ds(z0, nz + 2 * HALO), pl.ds(pl.multiple_of(x0 + PAD, 8), nx), :]
        mid = column[HALO : HALO + nz]
        flat = mid.reshape(nz * nx, length)
        high = flat.astype(BF16)
        low = (flat - high.astype(F32)).astype(BF16)
        lanes = jnp.dot(
            jnp.concatenate([high, low], axis=1), band[...], preferred_element_type=F32
        ).reshape(nz, nx, length)
        total = CENTER * mid + lanes
        planes = pl.ds(z0 + HALO, nz)
        for k in range(4):
            near = column[HALO + 1 + k : HALO + 1 + k + nz] + column[3 - k : 3 - k + nz]
            near = near + field[planes, pl.ds(x0 + PAD + 1 + k, nx), :]
            near = near + field[planes, pl.ds(x0 + PAD - 1 - k, nx), :]
            total = total + RINGS[k] * near
        return mid, total

    faces = ((0, HALO), (depth - HALO, HALO))
    middle = ((HALO, depth - 2 * HALO),)

    def sweep(blocks, work, unroll=UNROLL):
        def tile(j, carry):
            x0 = pl.multiple_of(j * TILE, TILE)
            for z0, nz in blocks:
                work(z0, nz, x0)
            return carry

        lax.fori_loop(0, width // TILE, tile, 0, unroll=unroll)

    def forward(t, now, prev):
        def work(z0, nz, x0):
            planes = pl.ds(z0, nz)
            rows = pl.ds(x0, TILE)
            at = (pl.ds(z0 + HALO, nz), pl.ds(pl.multiple_of(x0 + PAD, 8), TILE))
            mid, image = laplace(now, z0, nz, x0, TILE)
            value = (mid + mid - prev[at]) + cour_v[planes, rows] * image
            if t > 0:
                value = value + wavelet[t] * pattern[planes, rows]
            prev[at] = value
            if t == 0:
                image_0[planes, rows] = image
            elif t == 1:
                image_1[planes, rows] = image
            elif t == 2:
                grad[planes, rows] = image * a_4[planes, rows]
            else:
                grad[planes, rows] += image * a_5[planes, rows]

        return work

    def add_pattern(z0, nz, x0):
        at = (pl.ds(z0 + HALO, nz), pl.ds(pl.multiple_of(x0 + PAD, 8), TILE))
        u_b[at] += wavelet[0] * pattern[pl.ds(z0, nz), pl.ds(x0, TILE)]

    def adjoint(t, w_now, w_next, now, later, new):
        def work(z0, nz, x0):
            planes = pl.ds(z0, nz)
            rows = pl.ds(x0, TILE)
            _, along = laplace(w_now, z0, nz, x0, TILE)
            value = now[planes, rows]
            value = (value + value - later[planes, rows]) + along
            if t < steps - 1:
                value = value + inject[t, planes, rows]
                at = (pl.ds(z0 + HALO, nz), pl.ds(pl.multiple_of(x0 + PAD, 8), TILE))
                w_next[at] = cour_v[planes, rows] * value
            new[planes, rows] = value
            if t == 1:
                grad[planes, rows] += value * image_1[planes, rows]

        return work

    def add_inject(z0, nz, x0):
        planes = pl.ds(z0, nz)
        rows = pl.ds(x0, TILE)
        at = (pl.ds(z0 + HALO, nz), pl.ds(pl.multiple_of(x0 + PAD, 8), TILE))
        value = a_5[planes, rows] + inject[steps - 1, planes, rows]
        a_5[planes, rows] = value
        w_b[at] = cour_v[planes, rows] * value

    half = depth // 2

    def grad_copy(to, slot, part_no):
        return pltpu.make_async_remote_copy(
            src_ref=gsend.at[part_no, to],
            dst_ref=grecv.at[part_no, slot],
            send_sem=grad_send.at[part_no, to],
            recv_sem=grad_recv.at[part_no, slot],
            device_id={"enc": to},
            device_id_type=MESH,
        )

    def last_adjoint(part_no, blocks):
        def tile(i, carry):
            j = lax.rem(e + 1 + i, n)
            x0 = pl.multiple_of(j * 8, 8)
            rows = pl.ds(x0, 8)
            put = 0
            for z0, nz in blocks:
                planes = pl.ds(z0, nz)
                _, along = laplace(w_b, z0, nz, x0, 8)
                value = a_1[planes, rows]
                value = (value + value - a_4[planes, rows]) + along + inject[0, planes, rows]
                a_4[planes, rows] = value
                gsend[part_no, j, pl.ds(put, nz)] = (
                    grad[planes, rows] + value * image_0[planes, rows]
                )
                put += nz

            @pl.when(j != e)
            def _():
                grad_copy(j, e, part_no).start()

            return carry

        lax.fori_loop(0, n, tile, 0, unroll=LAST_UNROLL)

    loads[0].wait()
    loads[4].wait()
    loads[5].wait()
    work = forward(0, u_a, u_b)
    sweep(middle, work)
    halo_wait(0, fwd_now, u_a)
    sweep(faces, work)
    work = adjoint(3, w_a, w_b, a_4, a_5, a_5)
    sweep(middle, work)
    halo_wait(1, w_a, w_a)
    sweep(faces, work)

    lax.fori_loop(1, n, enc_wait, 0)
    pattern[...] = jnp.zeros(pattern.shape, F32)
    lax.fori_loop(0, n // group, sources, 0)
    sweep(faces, add_pattern)
    halo_start(2, u_b, u_b)
    sweep(middle, add_pattern)

    total = parts[0]
    for i in range(1, n):
        total = total + parts[i]
    traces_v[...] = total * (1.0 / (shots * n) ** 0.5)
    receivers(3)
    sweep(faces, add_inject)
    halo_start(3, w_b, w_b)
    sweep(middle, add_inject)
    for t in range(3):
        receivers(2 - t)

    halo_sent(0, fwd_now, u_a)
    work = forward(1, u_b, u_a)
    halo_wait(2, u_b, u_b)
    sweep(faces, work)
    halo_start(4, u_a, u_a)
    sweep(middle, work)

    halo_sent(1, w_a, w_a)
    work = adjoint(2, w_b, w_a, a_5, a_4, a_4)
    halo_wait(3, w_b, w_b)
    sweep(faces, work)
    halo_start(5, w_a, w_a)
    sweep(middle, work)

    halo_sent(2, u_b, u_b)
    work = forward(2, u_a, u_b)
    halo_wait(4, u_a, u_a)
    sweep(faces, work)
    halo_start(6, u_b, u_b)
    sweep(middle, work)

    halo_sent(3, w_b, w_b)
    work = adjoint(1, w_a, w_b, a_4, a_5, a_1)
    halo_wait(5, w_a, w_a)
    sweep(faces, work)
    halo_start(7, w_b, w_b)
    sweep(middle, work)

    halo_sent(4, u_a, u_a)
    work = forward(3, u_b, u_a)
    sweep(middle, work)
    halo_wait(6, u_b, u_b)
    sweep(faces, work)
    store_u = pltpu.make_async_copy(u_a.at[inner, body_rows, :], fwd_last.at[0], store_sem.at[0])
    store_u.start()

    last_adjoint(0, middle)
    halo_wait(7, w_b, w_b)
    last_adjoint(1, faces)
    store_a = pltpu.make_async_copy(a_4, adj_first.at[0], store_sem.at[1])
    store_a.start()

    def grad_sum(part_no):
        def grad_wait(k, share):
            slot = lax.rem(e + k, n)
            grad_copy(slot, slot, part_no).wait_recv()
            return share + grecv[part_no, slot]

        return lax.fori_loop(1, n, grad_wait, gsend[part_no, e]) * (1.0 / (UNIT * steps * n))

    gout[pl.ds(HALO, half)] = grad_sum(0)
    share = grad_sum(1)
    gout[pl.ds(0, HALO)] = share[:HALO]
    gout[pl.ds(depth - HALO, HALO)] = share[HALO:]
    store_g = pltpu.make_async_copy(gout, gradient, store_sem.at[2])
    store_g.start()

    def finish(k, carry):
        enc_copy(k, False).wait_send()
        to = lax.rem(e + k, n)
        grad_copy(to, to, 0).wait_send()
        grad_copy(to, to, 1).wait_send()
        return carry

    lax.fori_loop(1, n, finish, 0)
    halo_sent(5, w_a, w_a)
    halo_sent(6, u_b, u_b)
    halo_sent(7, w_b, w_b)
    store_u.wait()
    store_a.wait()
    store_g.wait()


def body(
    n,
    nd,
    residual,
    weights,
    source_pos,
    receiver_pos,
    wavelet,
    courant,
    fwd_prev,
    fwd_now,
    adj_next,
    adj_now,
):
    shots, steps, recvs = residual.shape
    depth, width, length = courant.shape
    share = (depth, width // n, length)
    field = pltpu.VMEM((depth, width, length), F32)
    padded = pltpu.VMEM((depth + 2 * HALO, width + 2 * PAD, length), F32)
    hot = max(2 * recvs, 4 * shots)
    anywhere = pl.BlockSpec(memory_space=pl.ANY)
    vmem = pl.BlockSpec(memory_space=pltpu.VMEM)
    return pl.pallas_call(
        functools.partial(kernel, n, nd),
        out_shape=(
            jax.ShapeDtypeStruct(share, F32),
            jax.ShapeDtypeStruct((1, depth, width, length), F32),
            jax.ShapeDtypeStruct((1, depth, width, length), F32),
        ),
        in_specs=[
            anywhere,
            vmem,
            vmem,
            vmem,
            pl.BlockSpec(memory_space=pltpu.SMEM),
            anywhere,
            anywhere,
            anywhere,
            anywhere,
            anywhere,
        ],
        out_specs=(anywhere, anywhere, anywhere),
        scratch_shapes=[
            pltpu.VMEM((shots, steps, recvs), BF16),
            field,
            padded,
            padded,
            padded,
            padded,
            field,
            field,
            field,
            field,
            field,
            field,
            field,
            pltpu.VMEM((steps, depth, width, length), F32),
            pltpu.VMEM((2 * length, length), BF16),
            pltpu.VMEM((n // 4, 4 * width, 4 * shots), BF16),
            pltpu.VMEM((4 * width, 2 * recvs), BF16),
            pltpu.VMEM((4 * length, hot), BF16),
            pltpu.VMEM((n, 8, recvs), F32),
            pltpu.VMEM((n, 8, recvs), F32),
            pltpu.VMEM((8, recvs), F32),
            pltpu.VMEM((2, n, depth // 2) + share[1:], F32),
            pltpu.VMEM((2, n, depth // 2) + share[1:], F32),
            pltpu.VMEM(share, F32),
            pltpu.SemaphoreType.DMA((6,)),
            pltpu.SemaphoreType.DMA((3,)),
            pltpu.SemaphoreType.DMA((n,)),
            pltpu.SemaphoreType.DMA((n,)),
            pltpu.SemaphoreType.DMA((8, 2)),
            pltpu.SemaphoreType.DMA((8, 2)),
            pltpu.SemaphoreType.DMA((2, n)),
            pltpu.SemaphoreType.DMA((2, n)),
        ],
        compiler_params=pltpu.CompilerParams(
            collective_id=0, has_side_effects=True, vmem_limit_bytes=56 * 2**20
        ),
    )(
        residual,
        weights,
        source_pos.reshape(n, 1, shots),
        receiver_pos.reshape(1, recvs),
        wavelet,
        courant,
        fwd_prev,
        fwd_now,
        adj_next,
        adj_now,
    )


def solution(mesh):
    placed = (
        P("enc", None, "dom"),
        P(None, "enc"),
        P(),
        P("dom"),
        P(),
        P("dom", None, None),
        P("enc", "dom", None, None),
        P("enc", "dom", None, None),
        P("enc", "dom", None, None),
        P("enc", "dom", None, None),
    )
    return jax.shard_map(
        functools.partial(body, mesh.shape["enc"], mesh.shape["dom"]),
        mesh=mesh,
        in_specs=placed,
        out_specs=(P("dom", "enc", None), P("enc", "dom", None, None), P("enc", "dom", None, None)),
        check_vma=False,
    )
```

```python
import functools

import jax
import jax.numpy as jnp
from jax import lax
from jax.experimental import pallas as pl
from jax.experimental.pallas import tpu as pltpu
from jax.sharding import PartitionSpec as P

MESH = pl.DeviceIdType.MESH
F32 = jnp.float32
BF16 = jnp.bfloat16
UNIT = 5040.0
CENTER = 3.0 * -14350.0
RINGS = (8064.0, -1008.0, 128.0, -9.0)
PAD = 8
HALO = 4
TILE = 16
UNROLL = 4
LAST_UNROLL = 4


def kernel(
    n,
    nd,
    residual,
    weights,
    source_pos,
    receiver_pos,
    wavelet,
    courant,
    fwd_prev,
    fwd_now,
    adj_next,
    adj_now,
    gradient,
    fwd_last,
    adj_first,
    res_v,
    cour_v,
    u_a,
    u_b,
    w_a,
    w_b,
    a_4,
    a_5,
    a_1,
    image_0,
    image_1,
    grad,
    pattern,
    inject,
    band,
    src_rows,
    recv_rows,
    cols_hot,
    part,
    parts,
    traces_v,
    gsend,
    gfirst,
    gsum,
    glast,
    fsend,
    frecv,
    staged,
    landed,
    load_sem,
    enc_send,
    enc_recv,
    halo_send,
    halo_recv,
    first_send,
    first_recv,
    last_send,
    last_recv,
    face_send,
    face_recv,
):
    depth, width, length = cour_v.shape
    shots = weights.shape[1]
    steps = res_v.shape[1]
    recvs = receiver_pos.shape[1]
    shift = width.bit_length() - 1
    e = lax.axis_index("enc")
    d = lax.axis_index("dom")
    inner = pl.ds(HALO, depth)
    body_rows = pl.ds(PAD, width)

    loads = [
        pltpu.make_async_copy(fwd_now.at[0], u_a.at[inner, body_rows, :], load_sem.at[0]),
        pltpu.make_async_copy(adj_now.at[0], a_4, load_sem.at[1]),
        pltpu.make_async_copy(courant, cour_v, load_sem.at[2]),
        pltpu.make_async_copy(residual, res_v, load_sem.at[3]),
        pltpu.make_async_copy(fwd_prev.at[0], u_b.at[inner, body_rows, :], load_sem.at[4]),
        pltpu.make_async_copy(adj_next.at[0], a_5, load_sem.at[5]),
    ]
    for copy in loads:
        copy.start()

    barrier = pltpu.get_barrier_semaphore()

    def greet(k, carry):
        pl.semaphore_signal(
            barrier, inc=1, device_id={"enc": lax.rem(e + k, n)}, device_id_type=MESH
        )
        return carry

    lax.fori_loop(1, n, greet, 0)

    @pl.when(d > 0)
    def _():
        pl.semaphore_signal(barrier, inc=1, device_id={"dom": d - 1}, device_id_type=MESH)

    @pl.when(d < nd - 1)
    def _():
        pl.semaphore_signal(barrier, inc=1, device_id={"dom": d + 1}, device_id_type=MESH)

    for field in (u_a, u_b, w_a, w_b):
        edge = jnp.zeros((depth + 2 * HALO, PAD, length), F32)
        field[:, pl.ds(0, PAD), :] = edge
        field[:, pl.ds(PAD + width, PAD), :] = edge

        @pl.when(d == 0)
        def _():
            field[pl.ds(0, HALO)] = jnp.zeros((HALO, width + 2 * PAD, length), F32)

        @pl.when(d == nd - 1)
        def _():
            field[pl.ds(HALO + depth, HALO)] = jnp.zeros((HALO, width + 2 * PAD, length), F32)

    loads[1].wait()
    loads[2].wait()

    def scale_tile(j, carry):
        rows = pl.ds(pl.multiple_of(j * 8, 8), 8)
        scaled = cour_v[:, rows, :] * (1.0 / UNIT)
        cour_v[:, rows, :] = scaled
        w_a[inner, pl.ds(pl.multiple_of(j * 8 + PAD, 8), 8), :] = scaled * a_4[:, rows, :]
        return carry

    lax.fori_loop(0, width // 8, scale_tile, 0)

    def halo_copies(h, field, down):
        way = 0 if down else 1
        to = {"dom": d - 1 if down else d + 1}
        face = field.at[HALO if down else HALO + depth - 1, body_rows, :]
        land = field.at[HALO + depth if down else HALO - 1, body_rows, :]
        return (
            pltpu.make_async_remote_copy(
                src_ref=face,
                dst_ref=land,
                send_sem=halo_send.at[h, way, 0],
                recv_sem=halo_recv.at[h, way, 0],
                device_id=to,
                device_id_type=MESH,
            ),
            pltpu.make_async_remote_copy(
                src_ref=staged.at[h, way],
                dst_ref=landed.at[h, way],
                send_sem=halo_send.at[h, way, 1],
                recv_sem=halo_recv.at[h, way, 1],
                device_id=to,
                device_id_type=MESH,
            ),
        )

    def halo_stage(h, field):
        staged[h, 0] = field[pl.ds(HALO + 1, HALO - 1), body_rows, :].astype(BF16)
        staged[h, 1] = field[pl.ds(depth, HALO - 1), body_rows, :].astype(BF16)

    def halo_start(h, field, stage=True):
        if stage:
            halo_stage(h, field)

        @pl.when(d > 0)
        def _():
            for copy in halo_copies(h, field, True):
                copy.start()

        @pl.when(d < nd - 1)
        def _():
            for copy in halo_copies(h, field, False):
                copy.start()

    def halo_sent(h, field):
        @pl.when(d > 0)
        def _():
            for copy in halo_copies(h, field, True):
                copy.wait_send()

        @pl.when(d < nd - 1)
        def _():
            for copy in halo_copies(h, field, False):
                copy.wait_send()

    def halo_wait(h, field):
        @pl.when(d < nd - 1)
        def _():
            for copy in halo_copies(h, field, True):
                copy.wait_recv()
            field[pl.ds(HALO + depth + 1, HALO - 1), body_rows, :] = landed[h, 0].astype(F32)

        @pl.when(d > 0)
        def _():
            for copy in halo_copies(h, field, False):
                copy.wait_recv()
            field[pl.ds(0, HALO - 1), body_rows, :] = landed[h, 1].astype(F32)

    loads[0].wait()
    halo_stage(0, u_a)
    halo_stage(1, w_a)
    pl.semaphore_wait(
        barrier, n - 1 + (d > 0).astype(jnp.int32) + (d < nd - 1).astype(jnp.int32)
    )

    halo_start(0, u_a, False)
    halo_start(1, w_a, False)

    signs = weights[...].astype(F32)
    shot_of = lax.shift_right_logical(lax.broadcasted_iota(jnp.int32, (shots, shots * steps), 1), 2)
    spread = jnp.where(
        shot_of == lax.broadcasted_iota(jnp.int32, (shots, shots * steps), 0), 1.0, 0.0
    ).astype(BF16)
    wide = jnp.dot(signs.astype(BF16), spread, preferred_element_type=F32)
    wide = jnp.broadcast_to(wide[:, None, :], (n, 8, shots * steps))
    same_step = (
        lax.broadcasted_iota(jnp.int32, (n, 8, shots * steps), 2) & (steps - 1)
    ) == lax.broadcasted_iota(jnp.int32, (n, 8, shots * steps), 1)
    wide = jnp.where(same_step, wide, 0.0).reshape(n * 8, shots * steps).astype(BF16)
    loads[3].wait()
    traces = jnp.dot(
        wide, res_v[...].reshape(shots * steps, recvs), preferred_element_type=F32
    )
    part[...] = traces.reshape(n, 8, recvs)
    part[:, steps, pl.ds(0, shots)] = signs
    parts[e] = part[e]

    def enc_copy(k, incoming):
        to = lax.rem(e + k, n)
        slot = lax.rem(e - k + n, n) if incoming else e
        return pltpu.make_async_remote_copy(
            src_ref=part.at[to],
            dst_ref=parts.at[slot],
            send_sem=enc_send.at[k],
            recv_sem=enc_recv.at[k],
            device_id={"enc": to},
            device_id_type=MESH,
        )

    def enc_start(k, carry):
        enc_copy(k, False).start()
        return carry

    lax.fori_loop(1, n, enc_start, 0)

    across = lax.broadcasted_iota(jnp.int32, (2 * length, length), 0) & (length - 1)
    gap = jnp.abs(across - lax.broadcasted_iota(jnp.int32, (2 * length, length), 1))
    weight = jnp.zeros((2 * length, length), F32)
    for k in range(4):
        weight = jnp.where(gap == k + 1, RINGS[k], weight)
    band[...] = weight.astype(BF16)

    base = d * (depth * width * length)
    hot_rows = 4 * width
    hot_cols = 4 * length

    def row_of(cell):
        return (lax.shift_right_arithmetic(cell, shift + 9) << shift) | (
            lax.shift_right_arithmetic(cell, 7) & (width - 1)
        )

    def col_of(cell):
        return ((lax.shift_right_arithmetic(cell, shift + 7) & 3) << 7) | (cell & 127)

    def enc_wait(k, carry):
        enc_copy(k, True).wait_recv()
        return carry

    def source_rows(i, carry):
        cell = source_pos[i] - base
        src_rows[:, pl.ds(pl.multiple_of(i * shots, shots), shots)] = jnp.where(
            lax.broadcasted_iota(jnp.int32, (hot_rows, shots), 0) == row_of(cell), 1.0, 0.0
        ).astype(BF16)
        return carry

    lax.fori_loop(0, n, source_rows, 0)
    recv_cell = receiver_pos[...] - base
    row_hot = jnp.where(
        lax.broadcasted_iota(jnp.int32, (hot_rows, recvs), 0) == row_of(recv_cell), 1.0, 0.0
    ).astype(BF16)
    recv_rows[:, pl.ds(0, recvs)] = row_hot
    recv_rows[:, pl.ds(recvs, recvs)] = row_hot

    def spread_out(rows, cols):
        return lax.dot_general(
            rows, cols, (((1,), (1,)), ((), ())), preferred_element_type=F32
        )

    def source_cols(i, carry):
        cell = source_pos[i] - base
        sign = parts[i, steps : steps + 1, pl.ds(0, shots)]
        cols_hot[:, pl.ds(pl.multiple_of(i * shots, shots), shots)] = jnp.where(
            lax.broadcasted_iota(jnp.int32, (hot_cols, shots), 0) == col_of(cell), sign, 0.0
        ).astype(BF16)
        return carry

    def sources():
        lax.fori_loop(0, n, source_cols, 0)
        placed = spread_out(src_rows[...], cols_hot[:, pl.ds(0, n * shots)])
        for q in range(4):
            for r in range(4):
                pattern[q * 4 + r] = placed[
                    q * width : (q + 1) * width, r * length : (r + 1) * length
                ]

    def receivers(t):
        value = traces_v[t : t + 1, :]
        high = value.astype(BF16).astype(F32)
        hit = lax.broadcasted_iota(jnp.int32, (hot_cols, recvs), 0) == col_of(recv_cell)
        cols_hot[:, pl.ds(0, recvs)] = jnp.where(hit, high, 0.0).astype(BF16)
        cols_hot[:, pl.ds(recvs, recvs)] = jnp.where(hit, value - high, 0.0).astype(BF16)
        placed = spread_out(recv_rows[...], cols_hot[:, pl.ds(0, 2 * recvs)])
        for q in range(4):
            for r in range(4):
                inject[t, q * 4 + r] = placed[
                    q * width : (q + 1) * width, r * length : (r + 1) * length
                ]

    def laplace(field, z0, nz, x0, nx):
        column = field[pl.ds(z0, nz + 2 * HALO), pl.ds(pl.multiple_of(x0 + PAD, 8), nx), :]
        mid = column[HALO : HALO + nz]
        flat = mid.reshape(nz * nx, length)
        high = flat.astype(BF16)
        low = (flat - high.astype(F32)).astype(BF16)
        lanes = jnp.dot(
            jnp.concatenate([high, low], axis=1), band[...], preferred_element_type=F32
        ).reshape(nz, nx, length)
        total = CENTER * mid + lanes
        planes = pl.ds(z0 + HALO, nz)
        for k in range(4):
            near = column[HALO + 1 + k : HALO + 1 + k + nz] + column[3 - k : 3 - k + nz]
            near = near + field[planes, pl.ds(x0 + PAD + 1 + k, nx), :]
            near = near + field[planes, pl.ds(x0 + PAD - 1 - k, nx), :]
            total = total + RINGS[k] * near
        return mid, total

    faces = ((0, HALO), (depth - HALO, HALO))
    middle = ((HALO, depth - 2 * HALO),)

    def sweep(blocks, work, unroll=UNROLL):
        def tile(j, carry):
            x0 = pl.multiple_of(j * TILE, TILE)
            for z0, nz in blocks:
                work(z0, nz, x0)
            return carry

        lax.fori_loop(0, width // TILE, tile, 0, unroll=unroll)

    def forward(t, now, prev):
        def work(z0, nz, x0):
            planes = pl.ds(z0, nz)
            rows = pl.ds(x0, TILE)
            at = (pl.ds(z0 + HALO, nz), pl.ds(pl.multiple_of(x0 + PAD, 8), TILE))
            mid, image = laplace(now, z0, nz, x0, TILE)
            value = (mid + mid - prev[at]) + cour_v[planes, rows] * image
            if t > 0:
                value = value + wavelet[t] * pattern[planes, rows]
            if t < steps - 1:
                prev[at] = value
            else:
                fwd_last[0, planes, rows] = value
            if t == 0:
                image_0[planes, rows] = image
            elif t == 1:
                image_1[planes, rows] = image
            elif t == 2:
                grad[planes, rows] = image * a_4[planes, rows]
            else:
                grad[planes, rows] += image * a_5[planes, rows]

        return work

    def add_pattern(z0, nz, x0):
        at = (pl.ds(z0 + HALO, nz), pl.ds(pl.multiple_of(x0 + PAD, 8), TILE))
        u_b[at] += wavelet[0] * pattern[pl.ds(z0, nz), pl.ds(x0, TILE)]

    def adjoint(t, w_now, w_next, now, later, new):
        def work(z0, nz, x0):
            planes = pl.ds(z0, nz)
            rows = pl.ds(x0, TILE)
            _, along = laplace(w_now, z0, nz, x0, TILE)
            value = now[planes, rows]
            value = (value + value - later[planes, rows]) + along
            if t < steps - 1:
                value = value + inject[t, planes, rows]
                at = (pl.ds(z0 + HALO, nz), pl.ds(pl.multiple_of(x0 + PAD, 8), TILE))
                w_next[at] = cour_v[planes, rows] * value
            new[planes, rows] = value
            if t == 1:
                grad[planes, rows] += value * image_1[planes, rows]

        return work

    def add_inject(z0, nz, x0):
        planes = pl.ds(z0, nz)
        rows = pl.ds(x0, TILE)
        at = (pl.ds(z0 + HALO, nz), pl.ds(pl.multiple_of(x0 + PAD, 8), TILE))
        value = a_5[planes, rows] + inject[steps - 1, planes, rows]
        a_5[planes, rows] = value
        w_b[at] = cour_v[planes, rows] * value

    half = depth // 2
    side = 4
    e_y, e_x = e // side, lax.rem(e, side)
    mine = ((e_y, e_x), (e_x, e_y))

    def owner(way, p, q):
        return p * side + q if way == 0 else q * side + p

    def first_copy(way, to, slot):
        return pltpu.make_async_remote_copy(
            src_ref=gsend.at[way, to],
            dst_ref=gfirst.at[way, slot],
            send_sem=first_send.at[way, to],
            recv_sem=first_recv.at[way, slot],
            device_id={"enc": owner(way, to, mine[way][1])},
            device_id_type=MESH,
        )

    def last_copy(way, to, slot):
        return pltpu.make_async_remote_copy(
            src_ref=gsum.at[way, to],
            dst_ref=glast.at[way, slot],
            send_sem=last_send.at[way, to],
            recv_sem=last_recv.at[way, slot],
            device_id={"enc": owner(way, mine[way][0], to)},
            device_id_type=MESH,
        )

    def face_copy(to, slot):
        return pltpu.make_async_remote_copy(
            src_ref=fsend.at[to],
            dst_ref=frecv.at[slot],
            send_sem=face_send.at[to],
            recv_sem=face_recv.at[slot],
            device_id={"enc": to},
            device_id_type=MESH,
        )

    def last_adjoint(z0, nz, j):
        x0 = pl.multiple_of(j * 8, 8)
        rows = pl.ds(x0, 8)
        planes = pl.ds(z0, nz)
        _, along = laplace(w_b, z0, nz, x0, 8)
        value = a_1[planes, rows]
        value = (value + value - a_4[planes, rows]) + along + inject[0, planes, rows]
        adj_first[0, planes, rows] = value
        return grad[planes, rows] + value * image_0[planes, rows]

    def last_middle():
        for off in (2, 1, 3, 0):
            to = lax.rem(e_y + off, side)

            def tile(q, carry):
                value = last_adjoint(HALO, half, to * side + q)
                gsend[0, to, q] = value[: half // 2]
                gsend[1, q, to] = value[half // 2 :]
                return carry

            lax.fori_loop(0, side, tile, 0, unroll=LAST_UNROLL)
            if off != 0:
                first_copy(0, to, e_y).start()
        for off in (2, 1, 3):
            first_copy(1, lax.rem(e_x + off, side), e_x).start()

    def last_faces():
        def tile(i, carry):
            j = lax.rem(e + 1 + i, n)
            fsend[j, pl.ds(0, HALO)] = last_adjoint(0, HALO, j)
            fsend[j, pl.ds(HALO, HALO)] = last_adjoint(depth - HALO, HALO, j)

            @pl.when(j != e)
            def _():
                face_copy(j, e).start()

            return carry

        lax.fori_loop(0, n, tile, 0, unroll=LAST_UNROLL)

    def first_sum(way):
        p, q = mine[way]
        total = gsend[way, p]
        for off in range(1, side):
            slot = lax.rem(p + off, side)
            first_copy(way, slot, slot).wait_recv()
            total = total + gfirst[way, slot]
        gsum[way] = total
        for off in range(1, side):
            last_copy(way, lax.rem(q + off, side), q).start()

    scale = 1.0 / (UNIT * steps * n)

    def last_sum(way):
        q = mine[way][1]
        total = gsum[way, q]
        for off in range(1, side):
            slot = lax.rem(q + off, side)
            last_copy(way, slot, slot).wait_recv()
            total = total + glast[way, slot]
        gradient[pl.ds(HALO + way * (half // 2), half // 2)] = total * scale

    def face_sum():
        def add(k, total):
            slot = lax.rem(e + k, n)
            face_copy(slot, slot).wait_recv()
            return total + frecv[slot]

        total = lax.fori_loop(1, n, add, fsend[e]) * scale
        gradient[pl.ds(0, HALO)] = total[:HALO]
        gradient[pl.ds(depth - HALO, HALO)] = total[HALO:]

    loads[4].wait()
    loads[5].wait()
    work = forward(0, u_a, u_b)
    sweep(middle, work)
    halo_wait(0, u_a)
    sweep(faces, work)
    work = adjoint(3, w_a, w_b, a_4, a_5, a_5)
    sweep(middle, work)
    halo_wait(1, w_a)
    sweep(faces, work)

    lax.fori_loop(1, n, enc_wait, 0)
    sources()
    sweep(faces, add_pattern)
    halo_start(2, u_b)
    sweep(middle, add_pattern)

    total = parts[0]
    for i in range(1, n):
        total = total + parts[i]
    traces_v[...] = total * (1.0 / (shots * n) ** 0.5)
    receivers(3)
    sweep(faces, add_inject)
    halo_start(3, w_b)
    sweep(middle, add_inject)
    for t in range(3):
        receivers(2 - t)

    halo_sent(0, u_a)
    work = forward(1, u_b, u_a)
    halo_wait(2, u_b)
    sweep(faces, work)
    halo_start(4, u_a)
    sweep(middle, work)

    halo_sent(1, w_a)
    work = adjoint(2, w_b, w_a, a_5, a_4, a_4)
    halo_wait(3, w_b)
    sweep(faces, work)
    halo_start(5, w_a)
    sweep(middle, work)

    halo_sent(2, u_b)
    work = forward(2, u_a, u_b)
    halo_wait(4, u_a)
    sweep(faces, work)
    halo_start(6, u_b)
    sweep(middle, work)

    halo_sent(3, w_b)
    work = adjoint(1, w_a, w_b, a_4, a_5, a_1)
    halo_wait(5, w_a)
    sweep(faces, work)
    halo_start(7, w_b)
    sweep(middle, work)

    halo_sent(4, u_a)
    work = forward(3, u_b, u_a)
    sweep(middle, work)
    halo_wait(6, u_b)
    sweep(faces, work)

    last_middle()
    halo_wait(7, w_b)
    last_faces()
    first_sum(0)
    first_sum(1)
    face_sum()
    last_sum(0)
    last_sum(1)

    def finish(k, carry):
        enc_copy(k, False).wait_send()
        to = lax.rem(e + k, n)
        face_copy(to, to).wait_send()
        return carry

    lax.fori_loop(1, n, finish, 0)
    for way in range(2):
        for off in range(1, side):
            to = lax.rem(mine[way][0] + off, side)
            first_copy(way, to, to).wait_send()
            to = lax.rem(mine[way][1] + off, side)
            last_copy(way, to, to).wait_send()
    halo_sent(5, w_a)
    halo_sent(6, u_b)
    halo_sent(7, w_b)


def store(share, fwd, adj, gradient, fwd_last, adj_first, sem):
    copies = [
        pltpu.make_async_copy(share, gradient, sem.at[0]),
        pltpu.make_async_copy(fwd, fwd_last, sem.at[1]),
        pltpu.make_async_copy(adj, adj_first, sem.at[2]),
    ]
    for copy in copies:
        copy.start()
    for copy in copies:
        copy.wait()


def body(
    n,
    nd,
    residual,
    weights,
    source_pos,
    receiver_pos,
    wavelet,
    courant,
    fwd_prev,
    fwd_now,
    adj_next,
    adj_now,
):
    shots, steps, recvs = residual.shape
    depth, width, length = courant.shape
    share = (depth, width // n, length)
    field = pltpu.VMEM((depth, width, length), F32)
    padded = pltpu.VMEM((depth + 2 * HALO, width + 2 * PAD, length), F32)
    hot = max(2 * recvs, n * shots)
    anywhere = pl.BlockSpec(memory_space=pl.ANY)
    vmem = pl.BlockSpec(memory_space=pltpu.VMEM)
    results = pl.pallas_call(
        functools.partial(kernel, n, nd),
        out_shape=(
            pltpu.VMEM(share, F32),
            pltpu.VMEM((1, depth, width, length), F32),
            pltpu.VMEM((1, depth, width, length), F32),
        ),
        in_specs=[
            anywhere,
            vmem,
            vmem,
            vmem,
            pl.BlockSpec(memory_space=pltpu.SMEM),
            anywhere,
            anywhere,
            anywhere,
            anywhere,
            anywhere,
        ],
        out_specs=(vmem, vmem, vmem),
        scratch_shapes=[
            pltpu.VMEM((shots, steps, recvs), BF16),
            field,
            padded,
            padded,
            padded,
            padded,
            field,
            field,
            field,
            field,
            field,
            field,
            field,
            pltpu.VMEM((steps, depth, width, length), F32),
            pltpu.VMEM((2 * length, length), BF16),
            pltpu.VMEM((4 * width, n * shots), BF16),
            pltpu.VMEM((4 * width, 2 * recvs), BF16),
            pltpu.VMEM((4 * length, hot), BF16),
            pltpu.VMEM((n, 8, recvs), F32),
            pltpu.VMEM((n, 8, recvs), F32),
            pltpu.VMEM((8, recvs), F32),
            pltpu.VMEM((2, 4, 4, depth // 4) + share[1:], F32),
            pltpu.VMEM((2, 4, 4, depth // 4) + share[1:], F32),
            pltpu.VMEM((2, 4, depth // 4) + share[1:], F32),
            pltpu.VMEM((2, 4, depth // 4) + share[1:], F32),
            pltpu.VMEM((n, depth // 2) + share[1:], F32),
            pltpu.VMEM((n, depth // 2) + share[1:], F32),
            pltpu.VMEM((8, 2, HALO - 1, width, length), BF16),
            pltpu.VMEM((8, 2, HALO - 1, width, length), BF16),
            pltpu.SemaphoreType.DMA((6,)),
            pltpu.SemaphoreType.DMA((n,)),
            pltpu.SemaphoreType.DMA((n,)),
            pltpu.SemaphoreType.DMA((8, 2, 2)),
            pltpu.SemaphoreType.DMA((8, 2, 2)),
            pltpu.SemaphoreType.DMA((2, 4)),
            pltpu.SemaphoreType.DMA((2, 4)),
            pltpu.SemaphoreType.DMA((2, 4)),
            pltpu.SemaphoreType.DMA((2, 4)),
            pltpu.SemaphoreType.DMA((n,)),
            pltpu.SemaphoreType.DMA((n,)),
        ],
        compiler_params=pltpu.CompilerParams(
            collective_id=0, has_side_effects=True, vmem_limit_bytes=58 * 2**20
        ),
    )(
        residual,
        weights,
        source_pos.reshape(n, 1, shots),
        receiver_pos.reshape(1, recvs),
        wavelet,
        courant,
        fwd_prev,
        fwd_now,
        adj_next,
        adj_now,
    )
    return pl.pallas_call(
        store,
        out_shape=tuple(jax.ShapeDtypeStruct(r.shape, F32) for r in results),
        in_specs=[vmem] * 3,
        out_specs=(anywhere,) * 3,
        scratch_shapes=[pltpu.SemaphoreType.DMA((3,))],
        compiler_params=pltpu.CompilerParams(vmem_limit_bytes=4 * 2**20),
    )(*results)


def solution(mesh):
    placed = (
        P("enc", None, "dom"),
        P(None, "enc"),
        P(),
        P("dom"),
        P(),
        P("dom", None, None),
        P("enc", "dom", None, None),
        P("enc", "dom", None, None),
        P("enc", "dom", None, None),
        P("enc", "dom", None, None),
    )
    return jax.shard_map(
        functools.partial(body, mesh.shape["enc"], mesh.shape["dom"]),
        mesh=mesh,
        in_specs=placed,
        out_specs=(P("dom", "enc", None), P("enc", "dom", None, None), P("enc", "dom", None, None)),
        check_vma=False,
    )
```

```python
import functools
import math

import jax
import jax.numpy as jnp
from jax import lax
from jax.experimental import pallas as pl
from jax.experimental.pallas import tpu as pltpu
from jax.sharding import PartitionSpec as P

MESH = pl.DeviceIdType.MESH
F32 = jnp.float32
BF16 = jnp.bfloat16
UNIT = 5040.0
CENTER = 3.0 * -14350.0
RINGS = (8064.0, -1008.0, 128.0, -9.0)
PAD = 8
HALO = 4
TILE = 16
UNROLL = 8


def kernel(
    n,
    nd,
    residual,
    weights,
    source_pos,
    receiver_pos,
    wavelet,
    courant,
    fwd_prev,
    fwd_now,
    adj_next,
    adj_now,
    gradient,
    fwd_last,
    adj_first,
    res_v,
    cour_v,
    u_a,
    u_b,
    w_a,
    w_b,
    a_4,
    a_5,
    a_1,
    image_0,
    image_1,
    grad,
    pattern,
    inject,
    band,
    src_rows,
    recv_rows,
    cols_hot,
    part,
    parts,
    traces_v,
    sign_out,
    sign_in,
    gsend,
    gfirst,
    gsum,
    glast,
    staged,
    landed,
    load_sem,
    enc_send,
    enc_recv,
    sign_send,
    sign_recv,
    halo_send,
    halo_recv,
    first_send,
    first_recv,
    last_send,
    last_recv,
):
    depth, width, length = cour_v.shape
    shots = weights.shape[1]
    steps = res_v.shape[1]
    recvs = receiver_pos.shape[1]
    shift = width.bit_length() - 1
    e = lax.axis_index("enc")
    d = lax.axis_index("dom")
    inner = pl.ds(HALO, depth)
    body_rows = pl.ds(PAD, width)

    loads = [
        pltpu.make_async_copy(fwd_now.at[0], u_a.at[inner, body_rows, :], load_sem.at[0]),
        pltpu.make_async_copy(residual, res_v, load_sem.at[3]),
        pltpu.make_async_copy(adj_now.at[0], a_4, load_sem.at[1]),
        pltpu.make_async_copy(courant, cour_v, load_sem.at[2]),
        pltpu.make_async_copy(fwd_prev.at[0], u_b.at[inner, body_rows, :], load_sem.at[4]),
        pltpu.make_async_copy(adj_next.at[0], a_5, load_sem.at[5]),
    ]
    for copy in loads:
        copy.start()

    barrier = pltpu.get_barrier_semaphore()

    def greet(k, carry):
        pl.semaphore_signal(
            barrier, inc=1, device_id={"enc": lax.rem(e + k, n)}, device_id_type=MESH
        )
        return carry

    lax.fori_loop(1, n, greet, 0)

    @pl.when(d > 0)
    def _():
        pl.semaphore_signal(barrier, inc=1, device_id={"dom": d - 1}, device_id_type=MESH)

    @pl.when(d < nd - 1)
    def _():
        pl.semaphore_signal(barrier, inc=1, device_id={"dom": d + 1}, device_id_type=MESH)

    for field in (u_a, u_b, w_a, w_b):
        edge = jnp.zeros((depth + 2 * HALO, PAD, length), F32)
        field[:, pl.ds(0, PAD), :] = edge
        field[:, pl.ds(PAD + width, PAD), :] = edge

        @pl.when(d == 0)
        def _():
            field[pl.ds(0, HALO)] = jnp.zeros((HALO, width + 2 * PAD, length), F32)

        @pl.when(d == nd - 1)
        def _():
            field[pl.ds(HALO + depth, HALO)] = jnp.zeros((HALO, width + 2 * PAD, length), F32)

    def halo_copies(h, field, down):
        way = 0 if down else 1
        to = {"dom": d - 1 if down else d + 1}
        face = field.at[HALO if down else HALO + depth - 1, body_rows, :]
        land = field.at[HALO + depth if down else HALO - 1, body_rows, :]
        return (
            pltpu.make_async_remote_copy(
                src_ref=face,
                dst_ref=land,
                send_sem=halo_send.at[h, way, 0],
                recv_sem=halo_recv.at[h, way, 0],
                device_id=to,
                device_id_type=MESH,
            ),
            pltpu.make_async_remote_copy(
                src_ref=staged.at[h, way],
                dst_ref=landed.at[h, way],
                send_sem=halo_send.at[h, way, 1],
                recv_sem=halo_recv.at[h, way, 1],
                device_id=to,
                device_id_type=MESH,
            ),
        )

    def halo_stage(h, field):
        staged[h, 0] = field[pl.ds(HALO + 1, HALO - 1), body_rows, :].astype(BF16)
        staged[h, 1] = field[pl.ds(depth, HALO - 1), body_rows, :].astype(BF16)

    def halo_start(h, field, stage=True):
        if stage:
            halo_stage(h, field)

        @pl.when(d > 0)
        def _():
            for copy in halo_copies(h, field, True):
                copy.start()

        @pl.when(d < nd - 1)
        def _():
            for copy in halo_copies(h, field, False):
                copy.start()

    def halo_sent(h, field):
        @pl.when(d > 0)
        def _():
            for copy in halo_copies(h, field, True):
                copy.wait_send()

        @pl.when(d < nd - 1)
        def _():
            for copy in halo_copies(h, field, False):
                copy.wait_send()

    def halo_wait(h, field):
        @pl.when(d < nd - 1)
        def _():
            for copy in halo_copies(h, field, True):
                copy.wait_recv()
            field[pl.ds(HALO + depth + 1, HALO - 1), body_rows, :] = landed[h, 0].astype(F32)

        @pl.when(d > 0)
        def _():
            for copy in halo_copies(h, field, False):
                copy.wait_recv()
            field[pl.ds(0, HALO - 1), body_rows, :] = landed[h, 1].astype(F32)

    signs = weights[...].astype(F32)
    sign_out[...] = signs.reshape(n, 1, shots)
    sign_in[e] = sign_out[e]

    def sign_copy(k, incoming):
        to = lax.rem(e + k, n)
        slot = lax.rem(e - k + n, n) if incoming else e
        return pltpu.make_async_remote_copy(
            src_ref=sign_out.at[to],
            dst_ref=sign_in.at[slot],
            send_sem=sign_send.at[k],
            recv_sem=sign_recv.at[k],
            device_id={"enc": to},
            device_id_type=MESH,
        )

    def sign_start(k, carry):
        sign_copy(k, False).start()
        return carry

    def sign_wait(k, carry):
        sign_copy(k, True).wait_recv()
        return carry

    loads[0].wait()
    halo_stage(0, u_a)
    pl.semaphore_wait(
        barrier, n - 1 + (d > 0).astype(jnp.int32) + (d < nd - 1).astype(jnp.int32)
    )

    halo_start(0, u_a, False)
    lax.fori_loop(1, n, sign_start, 0)

    shot_of = lax.shift_right_logical(lax.broadcasted_iota(jnp.int32, (shots, shots * steps), 1), 2)
    spread = jnp.where(
        shot_of == lax.broadcasted_iota(jnp.int32, (shots, shots * steps), 0), 1.0, 0.0
    ).astype(BF16)
    wide = jnp.dot(signs.astype(BF16), spread, preferred_element_type=F32)
    wide = jnp.broadcast_to(wide[:, None, :], (n, 8, shots * steps))
    same_step = (
        lax.broadcasted_iota(jnp.int32, (n, 8, shots * steps), 2) & (steps - 1)
    ) == lax.broadcasted_iota(jnp.int32, (n, 8, shots * steps), 1)
    wide = jnp.where(same_step, wide, 0.0).reshape(n * 8, shots * steps).astype(BF16)
    loads[1].wait()
    traces = jnp.dot(
        wide, res_v[...].reshape(shots * steps, recvs), preferred_element_type=F32
    )
    part[...] = traces.reshape(n, 8, recvs)
    parts[e] = part[e]

    def enc_copy(k, incoming):
        to = lax.rem(e + k, n)
        slot = lax.rem(e - k + n, n) if incoming else e
        return pltpu.make_async_remote_copy(
            src_ref=part.at[to, pl.ds(0, steps)],
            dst_ref=parts.at[slot, pl.ds(0, steps)],
            send_sem=enc_send.at[k],
            recv_sem=enc_recv.at[k],
            device_id={"enc": to},
            device_id_type=MESH,
        )

    def enc_start(k, carry):
        enc_copy(k, False).start()
        return carry

    lax.fori_loop(1, n, enc_start, 0)

    loads[2].wait()
    loads[3].wait()

    def scale_tile(j, carry):
        rows = pl.ds(pl.multiple_of(j * 8, 8), 8)
        scaled = cour_v[:, rows, :] * (1.0 / UNIT)
        cour_v[:, rows, :] = scaled
        w_a[inner, pl.ds(pl.multiple_of(j * 8 + PAD, 8), 8), :] = scaled * a_4[:, rows, :]
        return carry

    lax.fori_loop(0, width // 8, scale_tile, 0)
    halo_start(1, w_a)

    across = lax.broadcasted_iota(jnp.int32, (2 * length, length), 0) & (length - 1)
    gap = jnp.abs(across - lax.broadcasted_iota(jnp.int32, (2 * length, length), 1))
    weight = jnp.zeros((2 * length, length), F32)
    for k in range(4):
        weight = jnp.where(gap == k + 1, RINGS[k], weight)
    band[...] = weight.astype(BF16)

    base = d * (depth * width * length)
    hot_rows = 4 * width
    hot_cols = 4 * length

    def row_of(cell):
        return (lax.shift_right_arithmetic(cell, shift + 9) << shift) | (
            lax.shift_right_arithmetic(cell, 7) & (width - 1)
        )

    def col_of(cell):
        return ((lax.shift_right_arithmetic(cell, shift + 7) & 3) << 7) | (cell & 127)

    def enc_wait(k, carry):
        enc_copy(k, True).wait_recv()
        return carry

    def source_rows(i, carry):
        cell = source_pos[i] - base
        src_rows[:, pl.ds(pl.multiple_of(i * shots, shots), shots)] = jnp.where(
            lax.broadcasted_iota(jnp.int32, (hot_rows, shots), 0) == row_of(cell), 1.0, 0.0
        ).astype(BF16)
        return carry

    lax.fori_loop(0, n, source_rows, 0)
    recv_cell = receiver_pos[...] - base
    row_hot = jnp.where(
        lax.broadcasted_iota(jnp.int32, (hot_rows, recvs), 0) == row_of(recv_cell), 1.0, 0.0
    ).astype(BF16)
    recv_rows[:, pl.ds(0, recvs)] = row_hot
    recv_rows[:, pl.ds(recvs, recvs)] = row_hot

    def spread_out(rows, cols):
        return lax.dot_general(
            rows, cols, (((1,), (1,)), ((), ())), preferred_element_type=F32
        )

    def source_cols(i, carry):
        cell = source_pos[i] - base
        sign = sign_in[i]
        cols_hot[:, pl.ds(pl.multiple_of(i * shots, shots), shots)] = jnp.where(
            lax.broadcasted_iota(jnp.int32, (hot_cols, shots), 0) == col_of(cell), sign, 0.0
        ).astype(BF16)
        return carry

    def sources():
        lax.fori_loop(0, n, source_cols, 0)
        placed = spread_out(src_rows[...], cols_hot[:, pl.ds(0, n * shots)])
        for q in range(4):
            for r in range(4):
                pattern[q * 4 + r] = placed[
                    q * width : (q + 1) * width, r * length : (r + 1) * length
                ]

    def receivers(t):
        value = traces_v[t : t + 1, :]
        high = value.astype(BF16).astype(F32)
        hit = lax.broadcasted_iota(jnp.int32, (hot_cols, recvs), 0) == col_of(recv_cell)
        cols_hot[:, pl.ds(0, recvs)] = jnp.where(hit, high, 0.0).astype(BF16)
        cols_hot[:, pl.ds(recvs, recvs)] = jnp.where(hit, value - high, 0.0).astype(BF16)
        placed = spread_out(recv_rows[...], cols_hot[:, pl.ds(0, 2 * recvs)])
        for q in range(4):
            for r in range(4):
                inject[t, q * 4 + r] = placed[
                    q * width : (q + 1) * width, r * length : (r + 1) * length
                ]

    def laplace(field, z0, nz, x0, nx):
        column = field[pl.ds(z0, nz + 2 * HALO), pl.ds(pl.multiple_of(x0 + PAD, 8), nx), :]
        mid = column[HALO : HALO + nz]
        flat = mid.reshape(nz * nx, length)
        high = flat.astype(BF16)
        low = (flat - high.astype(F32)).astype(BF16)
        lanes = jnp.dot(
            jnp.concatenate([high, low], axis=1), band[...], preferred_element_type=F32
        ).reshape(nz, nx, length)
        total = CENTER * mid + lanes
        planes = pl.ds(z0 + HALO, nz)
        for k in range(4):
            near = column[HALO + 1 + k : HALO + 1 + k + nz] + column[3 - k : 3 - k + nz]
            near = near + field[planes, pl.ds(x0 + PAD + 1 + k, nx), :]
            near = near + field[planes, pl.ds(x0 + PAD - 1 - k, nx), :]
            total = total + RINGS[k] * near
        return mid, total

    faces = ((0, HALO), (depth - HALO, HALO))
    middle = ((HALO, depth - 2 * HALO),)

    def sweep(blocks, work, unroll=UNROLL):
        def tile(j, carry):
            x0 = pl.multiple_of(j * TILE, TILE)
            for z0, nz in blocks:
                work(z0, nz, x0)
            return carry

        lax.fori_loop(0, width // TILE, tile, 0, unroll=unroll)

    def forward(t, now, prev, bare=False):
        def work(z0, nz, x0):
            planes = pl.ds(z0, nz)
            rows = pl.ds(x0, TILE)
            at = (pl.ds(z0 + HALO, nz), pl.ds(pl.multiple_of(x0 + PAD, 8), TILE))
            mid, image = laplace(now, z0, nz, x0, TILE)
            value = (mid + mid - prev[at]) + cour_v[planes, rows] * image
            if not bare:
                value = value + wavelet[t] * pattern[planes, rows]
            if t < steps - 1:
                prev[at] = value
            else:
                fwd_last[0, planes, rows] = value
            if t == 0:
                image_0[planes, rows] = image
            elif t == 1:
                image_1[planes, rows] = image
            elif t == 2:
                grad[planes, rows] = image * a_4[planes, rows]
            else:
                grad[planes, rows] += image * a_5[planes, rows]

        return work

    def add_pattern(z0, nz, x0):
        at = (pl.ds(z0 + HALO, nz), pl.ds(pl.multiple_of(x0 + PAD, 8), TILE))
        u_b[at] += wavelet[0] * pattern[pl.ds(z0, nz), pl.ds(x0, TILE)]

    def adjoint(t, w_now, w_next, now, later, new, bare=False):
        def work(z0, nz, x0):
            planes = pl.ds(z0, nz)
            rows = pl.ds(x0, TILE)
            _, along = laplace(w_now, z0, nz, x0, TILE)
            value = now[planes, rows]
            value = (value + value - later[planes, rows]) + along
            if not bare:
                value = value + inject[t, planes, rows]
                at = (pl.ds(z0 + HALO, nz), pl.ds(pl.multiple_of(x0 + PAD, 8), TILE))
                w_next[at] = cour_v[planes, rows] * value
            new[planes, rows] = value
            if t == 1:
                grad[planes, rows] += value * image_1[planes, rows]

        return work

    def add_inject(z0, nz, x0):
        planes = pl.ds(z0, nz)
        rows = pl.ds(x0, TILE)
        at = (pl.ds(z0 + HALO, nz), pl.ds(pl.multiple_of(x0 + PAD, 8), TILE))
        value = a_5[planes, rows] + inject[steps - 1, planes, rows]
        a_5[planes, rows] = value
        w_b[at] = cour_v[planes, rows] * value

    half = depth // 2
    side = math.isqrt(n)
    e_y, e_x = e // side, lax.rem(e, side)
    mine = ((e_y, e_x), (e_x, e_y))

    def owner(way, p, q):
        return p * side + q if way == 0 else q * side + p

    def first_copy(group, way, to, slot):
        return pltpu.make_async_remote_copy(
            src_ref=gsend.at[group, way, to],
            dst_ref=gfirst.at[group, way, slot],
            send_sem=first_send.at[group, way, to],
            recv_sem=first_recv.at[group, way, slot],
            device_id={"enc": owner(way, to, mine[way][1])},
            device_id_type=MESH,
        )

    def last_copy(group, way, to, slot):
        return pltpu.make_async_remote_copy(
            src_ref=gsum.at[group, way, to],
            dst_ref=glast.at[group, way, slot],
            send_sem=last_send.at[group, way, to],
            recv_sem=last_recv.at[group, way, slot],
            device_id={"enc": owner(way, mine[way][0], to)},
            device_id_type=MESH,
        )

    span = side * 8

    def last_adjoint(z0, nz, x0, nx):
        rows = pl.ds(x0, nx)
        planes = pl.ds(z0, nz)
        _, along = laplace(w_b, z0, nz, x0, nx)
        value = a_1[planes, rows]
        value = (value + value - a_4[planes, rows]) + along + inject[0, planes, rows]
        adj_first[0, planes, rows] = value
        return grad[planes, rows] + value * image_0[planes, rows]

    others = (2, 1, 3) if side == 4 else tuple(range(1, side))

    def last_step(group):
        for off in others + (0,):
            to = lax.rem(e_y + off, side)

            for at in range(0, span, TILE):
                x0 = pl.multiple_of(to * span + at, 8)
                if group == 0:
                    value = last_adjoint(HALO, half, x0, TILE)
                    lower, upper = value[:HALO], value[HALO:]
                else:
                    lower = last_adjoint(0, HALO, x0, TILE)
                    upper = last_adjoint(depth - HALO, HALO, x0, TILE)
                for r in range(TILE // 8):
                    gsend[group, 0, to, at // 8 + r] = lower[:, r * 8 : r * 8 + 8]
                    gsend[group, 1, at // 8 + r, to] = upper[:, r * 8 : r * 8 + 8]
            if off != 0:
                first_copy(group, 0, to, e_y).start()
        for off in others:
            first_copy(group, 1, lax.rem(e_x + off, side), e_x).start()

    def first_sum(group, way):
        p, q = mine[way]
        total = gsend[group, way, p]
        for off in range(1, side):
            slot = lax.rem(p + off, side)
            first_copy(group, way, slot, slot).wait_recv()
            total = total + gfirst[group, way, slot]
        gsum[group, way] = total
        for off in others:
            last_copy(group, way, lax.rem(q + off, side), q).start()

    def last_sum(group, way):
        q = mine[way][1]
        total = gsum[group, way, q]
        for off in range(1, side):
            slot = lax.rem(q + off, side)
            last_copy(group, way, slot, slot).wait_recv()
            total = total + glast[group, way, slot]
        z0 = HALO * (1 + way) if group == 0 else way * (depth - HALO)
        gradient[pl.ds(z0, HALO)] = total * (1.0 / (UNIT * steps * n))

    loads[4].wait()
    loads[5].wait()
    sweep(middle, forward(0, u_a, u_b, True))
    sweep(middle, adjoint(3, w_a, None, a_4, a_5, a_5, True))
    lax.fori_loop(1, n, sign_wait, 0)
    sources()
    halo_wait(0, u_a)
    sweep(faces, forward(0, u_a, u_b))
    halo_start(2, u_b)
    lax.fori_loop(1, n, enc_wait, 0)
    total = parts[0, pl.ds(0, steps)]
    for i in range(1, n):
        total = total + parts[i, pl.ds(0, steps)]
    traces_v[...] = total * (1.0 / (shots * n) ** 0.5)
    receivers(3)
    halo_wait(1, w_a)
    sweep(faces, adjoint(3, w_a, w_b, a_4, a_5, a_5))
    halo_start(3, w_b)
    sweep(middle, add_pattern)
    sweep(middle, add_inject)
    for t in range(3):
        receivers(2 - t)

    halo_sent(0, u_a)
    work = forward(1, u_b, u_a)
    halo_wait(2, u_b)
    sweep(faces, work)
    halo_start(4, u_a)
    sweep(middle, work)

    halo_sent(1, w_a)
    work = adjoint(2, w_b, w_a, a_5, a_4, a_4)
    halo_wait(3, w_b)
    sweep(faces, work)
    halo_start(5, w_a)
    sweep(middle, work)

    halo_sent(2, u_b)
    work = forward(2, u_a, u_b)
    halo_wait(4, u_a)
    sweep(faces, work)
    halo_start(6, u_b)
    sweep(middle, work)

    halo_sent(3, w_b)
    work = adjoint(1, w_a, w_b, a_4, a_5, a_1)
    halo_wait(5, w_a)
    sweep(faces, work)
    halo_start(7, w_b)
    sweep(middle, work)

    halo_sent(4, u_a)
    work = forward(3, u_b, u_a)
    sweep(middle, work)
    halo_wait(6, u_b)
    sweep(faces, work)

    last_step(0)
    halo_wait(7, w_b)
    last_step(1)
    for group in range(2):
        for way in range(2):
            first_sum(group, way)
    for group in range(2):
        for way in range(2):
            last_sum(group, way)

    def finish(k, carry):
        enc_copy(k, False).wait_send()
        sign_copy(k, False).wait_send()
        return carry

    lax.fori_loop(1, n, finish, 0)
    for group in range(2):
        for way in range(2):
            for off in others:
                to = lax.rem(mine[way][0] + off, side)
                first_copy(group, way, to, to).wait_send()
                to = lax.rem(mine[way][1] + off, side)
                last_copy(group, way, to, to).wait_send()
    halo_sent(5, w_a)
    halo_sent(6, u_b)
    halo_sent(7, w_b)


def store(share, fwd, adj, gradient, fwd_last, adj_first, sem):
    copies = [
        pltpu.make_async_copy(share, gradient, sem.at[0]),
        pltpu.make_async_copy(fwd, fwd_last, sem.at[1]),
        pltpu.make_async_copy(adj, adj_first, sem.at[2]),
    ]
    for copy in copies:
        copy.start()
    for copy in copies:
        copy.wait()


def body(
    n,
    nd,
    residual,
    weights,
    source_pos,
    receiver_pos,
    wavelet,
    courant,
    fwd_prev,
    fwd_now,
    adj_next,
    adj_now,
):
    shots, steps, recvs = residual.shape
    depth, width, length = courant.shape
    share = (depth, width // n, length)
    side = math.isqrt(n)
    field = pltpu.VMEM((depth, width, length), F32)
    padded = pltpu.VMEM((depth + 2 * HALO, width + 2 * PAD, length), F32)
    hot = max(2 * recvs, n * shots)
    anywhere = pl.BlockSpec(memory_space=pl.ANY)
    vmem = pl.BlockSpec(memory_space=pltpu.VMEM)
    results = pl.pallas_call(
        functools.partial(kernel, n, nd),
        out_shape=(
            pltpu.VMEM(share, F32),
            pltpu.VMEM((1, depth, width, length), F32),
            pltpu.VMEM((1, depth, width, length), F32),
        ),
        in_specs=[
            anywhere,
            vmem,
            vmem,
            vmem,
            pl.BlockSpec(memory_space=pltpu.SMEM),
            anywhere,
            anywhere,
            anywhere,
            anywhere,
            anywhere,
        ],
        out_specs=(vmem, vmem, vmem),
        scratch_shapes=[
            pltpu.VMEM((shots, steps, recvs), BF16),
            field,
            padded,
            padded,
            padded,
            padded,
            field,
            field,
            field,
            field,
            field,
            field,
            field,
            pltpu.VMEM((steps, depth, width, length), F32),
            pltpu.VMEM((2 * length, length), BF16),
            pltpu.VMEM((4 * width, n * shots), BF16),
            pltpu.VMEM((4 * width, 2 * recvs), BF16),
            pltpu.VMEM((4 * length, hot), BF16),
            pltpu.VMEM((n, 8, recvs), F32),
            pltpu.VMEM((n, 8, recvs), F32),
            pltpu.VMEM((steps, recvs), F32),
            pltpu.VMEM((n, 1, shots), F32),
            pltpu.VMEM((n, 1, shots), F32),
            pltpu.VMEM((2, 2, side, side, HALO) + share[1:], F32),
            pltpu.VMEM((2, 2, side, side, HALO) + share[1:], F32),
            pltpu.VMEM((2, 2, side, HALO) + share[1:], F32),
            pltpu.VMEM((2, 2, side, HALO) + share[1:], F32),
            pltpu.VMEM((8, 2, HALO - 1, width, length), BF16),
            pltpu.VMEM((8, 2, HALO - 1, width, length), BF16),
            pltpu.SemaphoreType.DMA((6,)),
            pltpu.SemaphoreType.DMA((n,)),
            pltpu.SemaphoreType.DMA((n,)),
            pltpu.SemaphoreType.DMA((n,)),
            pltpu.SemaphoreType.DMA((n,)),
            pltpu.SemaphoreType.DMA((8, 2, 2)),
            pltpu.SemaphoreType.DMA((8, 2, 2)),
            pltpu.SemaphoreType.DMA((2, 2, side)),
            pltpu.SemaphoreType.DMA((2, 2, side)),
            pltpu.SemaphoreType.DMA((2, 2, side)),
            pltpu.SemaphoreType.DMA((2, 2, side)),
        ],
        compiler_params=pltpu.CompilerParams(
            collective_id=0, has_side_effects=True, vmem_limit_bytes=58 * 2**20
        ),
    )(
        residual,
        weights,
        source_pos.reshape(n, 1, shots),
        receiver_pos.reshape(1, recvs),
        wavelet,
        courant,
        fwd_prev,
        fwd_now,
        adj_next,
        adj_now,
    )
    return pl.pallas_call(
        store,
        out_shape=tuple(jax.ShapeDtypeStruct(r.shape, F32) for r in results),
        in_specs=[vmem] * 3,
        out_specs=(anywhere,) * 3,
        scratch_shapes=[pltpu.SemaphoreType.DMA((3,))],
        compiler_params=pltpu.CompilerParams(vmem_limit_bytes=4 * 2**20),
    )(*results)


def solution(mesh):
    placed = (
        P("enc", None, "dom"),
        P(None, "enc"),
        P(),
        P("dom"),
        P(),
        P("dom", None, None),
        P("enc", "dom", None, None),
        P("enc", "dom", None, None),
        P("enc", "dom", None, None),
        P("enc", "dom", None, None),
    )
    return jax.shard_map(
        functools.partial(body, mesh.shape["enc"], mesh.shape["dom"]),
        mesh=mesh,
        in_specs=placed,
        out_specs=(P("dom", "enc", None), P("enc", "dom", None, None), P("enc", "dom", None, None)),
        check_vma=False,
    )
```

```python
import functools
import math

import jax
import jax.numpy as jnp
from jax import lax
from jax.experimental import pallas as pl
from jax.experimental.pallas import tpu as pltpu
from jax.sharding import PartitionSpec as P

MESH = pl.DeviceIdType.MESH
F32 = jnp.float32
BF16 = jnp.bfloat16
UNIT = 5040.0
CENTER = 3.0 * -14350.0
RINGS = (8064.0, -1008.0, 128.0, -9.0)
PAD = 8
HALO = 4
TILE = 16
UNROLL = 8


def kernel(
    n,
    nd,
    residual,
    weights,
    source_pos,
    receiver_pos,
    wavelet,
    courant,
    fwd_prev,
    fwd_now,
    adj_next,
    adj_now,
    gradient,
    fwd_last,
    adj_first,
    res_v,
    cour_v,
    u_a,
    u_b,
    w_a,
    w_b,
    a_4,
    a_5,
    a_1,
    image_0,
    image_1,
    grad,
    pattern,
    inject,
    band,
    src_rows,
    recv_rows,
    cols_hot,
    part,
    parts,
    traces_v,
    sign_out,
    sign_in,
    gsend,
    gfirst,
    gsum,
    glast,
    staged,
    landed,
    load_sem,
    enc_send,
    enc_recv,
    sign_send,
    sign_recv,
    halo_send,
    halo_recv,
    first_send,
    first_recv,
    last_send,
    last_recv,
):
    depth, width, length = cour_v.shape
    shots = weights.shape[1]
    steps = res_v.shape[1]
    recvs = receiver_pos.shape[1]
    shift = width.bit_length() - 1
    e = lax.axis_index("enc")
    d = lax.axis_index("dom")
    inner = pl.ds(HALO, depth)
    body_rows = pl.ds(PAD, width)

    loads = [
        pltpu.make_async_copy(fwd_now.at[0], u_a.at[inner, body_rows, :], load_sem.at[0]),
        pltpu.make_async_copy(residual, res_v, load_sem.at[3]),
        pltpu.make_async_copy(adj_now.at[0], a_4, load_sem.at[1]),
        pltpu.make_async_copy(courant, cour_v, load_sem.at[2]),
        pltpu.make_async_copy(fwd_prev.at[0], u_b.at[inner, body_rows, :], load_sem.at[4]),
        pltpu.make_async_copy(adj_next.at[0], a_5, load_sem.at[5]),
    ]
    for copy in loads:
        copy.start()

    barrier = pltpu.get_barrier_semaphore()

    def greet(k, carry):
        pl.semaphore_signal(
            barrier, inc=1, device_id={"enc": lax.rem(e + k, n)}, device_id_type=MESH
        )
        return carry

    lax.fori_loop(1, n, greet, 0)

    @pl.when(d > 0)
    def _():
        pl.semaphore_signal(barrier, inc=1, device_id={"dom": d - 1}, device_id_type=MESH)

    @pl.when(d < nd - 1)
    def _():
        pl.semaphore_signal(barrier, inc=1, device_id={"dom": d + 1}, device_id_type=MESH)

    for field in (u_a, u_b, w_a, w_b):
        edge = jnp.zeros((depth + 2 * HALO, PAD, length), F32)
        field[:, pl.ds(0, PAD), :] = edge
        field[:, pl.ds(PAD + width, PAD), :] = edge

        @pl.when(d == 0)
        def _():
            field[pl.ds(0, HALO)] = jnp.zeros((HALO, width + 2 * PAD, length), F32)

        @pl.when(d == nd - 1)
        def _():
            field[pl.ds(HALO + depth, HALO)] = jnp.zeros((HALO, width + 2 * PAD, length), F32)

    rows_half = width // 2

    def halo_copies(h, field, down, part_no):
        way = 0 if down else 1
        to = {"dom": d - 1 if down else d + 1}
        rows = pl.ds(PAD + part_no * rows_half, rows_half)
        face = field.at[HALO if down else HALO + depth - 1, rows, :]
        land = field.at[HALO + depth if down else HALO - 1, rows, :]
        return (
            pltpu.make_async_remote_copy(
                src_ref=face,
                dst_ref=land,
                send_sem=halo_send.at[h, way, part_no, 0],
                recv_sem=halo_recv.at[h, way, part_no, 0],
                device_id=to,
                device_id_type=MESH,
            ),
            pltpu.make_async_remote_copy(
                src_ref=staged.at[h, way, part_no],
                dst_ref=landed.at[h, way, part_no],
                send_sem=halo_send.at[h, way, part_no, 1],
                recv_sem=halo_recv.at[h, way, part_no, 1],
                device_id=to,
                device_id_type=MESH,
            ),
        )

    def halo_stage(h, field, part_no):
        rows = pl.ds(PAD + part_no * rows_half, rows_half)
        staged[h, 0, part_no] = field[pl.ds(HALO + 1, HALO - 1), rows, :].astype(BF16)
        staged[h, 1, part_no] = field[pl.ds(depth, HALO - 1), rows, :].astype(BF16)

    def halo_start(h, field, part_no):
        @pl.when(d > 0)
        def _():
            for copy in halo_copies(h, field, True, part_no):
                copy.start()

        @pl.when(d < nd - 1)
        def _():
            for copy in halo_copies(h, field, False, part_no):
                copy.start()

    def halo_sent(h, field):
        for part_no in range(2):

            @pl.when(d > 0)
            def _():
                for copy in halo_copies(h, field, True, part_no):
                    copy.wait_send()

            @pl.when(d < nd - 1)
            def _():
                for copy in halo_copies(h, field, False, part_no):
                    copy.wait_send()

    def halo_wait(h, field):
        for part_no in range(2):
            rows = pl.ds(PAD + part_no * rows_half, rows_half)

            @pl.when(d < nd - 1)
            def _():
                for copy in halo_copies(h, field, True, part_no):
                    copy.wait_recv()
                field[pl.ds(HALO + depth + 1, HALO - 1), rows, :] = landed[h, 0, part_no].astype(F32)

            @pl.when(d > 0)
            def _():
                for copy in halo_copies(h, field, False, part_no):
                    copy.wait_recv()
                field[pl.ds(0, HALO - 1), rows, :] = landed[h, 1, part_no].astype(F32)

    signs = weights[...].astype(F32)
    sign_out[...] = signs.reshape(n, 1, shots)
    sign_in[e] = sign_out[e]

    def sign_copy(k, incoming):
        to = lax.rem(e + k, n)
        slot = lax.rem(e - k + n, n) if incoming else e
        return pltpu.make_async_remote_copy(
            src_ref=sign_out.at[to],
            dst_ref=sign_in.at[slot],
            send_sem=sign_send.at[k],
            recv_sem=sign_recv.at[k],
            device_id={"enc": to},
            device_id_type=MESH,
        )

    def sign_start(k, carry):
        sign_copy(k, False).start()
        return carry

    def sign_wait(k, carry):
        sign_copy(k, True).wait_recv()
        return carry

    loads[0].wait()
    halo_stage(0, u_a, 0)
    halo_stage(0, u_a, 1)
    pl.semaphore_wait(
        barrier, n - 1 + (d > 0).astype(jnp.int32) + (d < nd - 1).astype(jnp.int32)
    )

    halo_start(0, u_a, 0)
    halo_start(0, u_a, 1)
    lax.fori_loop(1, n, sign_start, 0)

    shot_of = lax.shift_right_logical(lax.broadcasted_iota(jnp.int32, (shots, shots * steps), 1), 2)
    spread = jnp.where(
        shot_of == lax.broadcasted_iota(jnp.int32, (shots, shots * steps), 0), 1.0, 0.0
    ).astype(BF16)
    wide = jnp.dot(signs.astype(BF16), spread, preferred_element_type=F32)
    wide = jnp.broadcast_to(wide[:, None, :], (n, 8, shots * steps))
    same_step = (
        lax.broadcasted_iota(jnp.int32, (n, 8, shots * steps), 2) & (steps - 1)
    ) == lax.broadcasted_iota(jnp.int32, (n, 8, shots * steps), 1)
    wide = jnp.where(same_step, wide, 0.0).reshape(n * 8, shots * steps).astype(BF16)
    loads[1].wait()
    traces = jnp.dot(
        wide, res_v[...].reshape(shots * steps, recvs), preferred_element_type=F32
    )
    part[...] = traces.reshape(n, 8, recvs)
    parts[e] = part[e]

    def enc_copy(k, incoming):
        to = lax.rem(e + k, n)
        slot = lax.rem(e - k + n, n) if incoming else e
        return pltpu.make_async_remote_copy(
            src_ref=part.at[to, pl.ds(0, steps)],
            dst_ref=parts.at[slot, pl.ds(0, steps)],
            send_sem=enc_send.at[k],
            recv_sem=enc_recv.at[k],
            device_id={"enc": to},
            device_id_type=MESH,
        )

    def enc_start(k, carry):
        enc_copy(k, False).start()
        return carry

    lax.fori_loop(1, n, enc_start, 0)

    loads[2].wait()
    loads[3].wait()

    def scale_tile(j, carry):
        rows = pl.ds(pl.multiple_of(j * 8, 8), 8)
        scaled = cour_v[:, rows, :] * (1.0 / UNIT)
        cour_v[:, rows, :] = scaled
        w_a[inner, pl.ds(pl.multiple_of(j * 8 + PAD, 8), 8), :] = scaled * a_4[:, rows, :]
        return carry

    lax.fori_loop(0, width // 8, scale_tile, 0)
    for part_no in range(2):
        halo_stage(1, w_a, part_no)
        halo_start(1, w_a, part_no)

    across = lax.broadcasted_iota(jnp.int32, (2 * length, length), 0) & (length - 1)
    gap = jnp.abs(across - lax.broadcasted_iota(jnp.int32, (2 * length, length), 1))
    weight = jnp.zeros((2 * length, length), F32)
    for k in range(4):
        weight = jnp.where(gap == k + 1, RINGS[k], weight)
    band[...] = weight.astype(BF16)

    base = d * (depth * width * length)
    hot_rows = 4 * width
    hot_cols = 4 * length

    def row_of(cell):
        return (lax.shift_right_arithmetic(cell, shift + 9) << shift) | (
            lax.shift_right_arithmetic(cell, 7) & (width - 1)
        )

    def col_of(cell):
        return ((lax.shift_right_arithmetic(cell, shift + 7) & 3) << 7) | (cell & 127)

    def enc_wait(k, carry):
        enc_copy(k, True).wait_recv()
        return carry

    def source_rows(i, carry):
        cell = source_pos[i] - base
        src_rows[:, pl.ds(pl.multiple_of(i * shots, shots), shots)] = jnp.where(
            lax.broadcasted_iota(jnp.int32, (hot_rows, shots), 0) == row_of(cell), 1.0, 0.0
        ).astype(BF16)
        return carry

    lax.fori_loop(0, n, source_rows, 0)
    recv_cell = receiver_pos[...] - base
    row_hot = jnp.where(
        lax.broadcasted_iota(jnp.int32, (hot_rows, recvs), 0) == row_of(recv_cell), 1.0, 0.0
    ).astype(BF16)
    recv_rows[:, pl.ds(0, recvs)] = row_hot
    recv_rows[:, pl.ds(recvs, recvs)] = row_hot

    def spread_out(rows, cols):
        return lax.dot_general(
            rows, cols, (((1,), (1,)), ((), ())), preferred_element_type=F32
        )

    def source_cols(i, carry):
        cell = source_pos[i] - base
        sign = sign_in[i]
        cols_hot[:, pl.ds(pl.multiple_of(i * shots, shots), shots)] = jnp.where(
            lax.broadcasted_iota(jnp.int32, (hot_cols, shots), 0) == col_of(cell), sign, 0.0
        ).astype(BF16)
        return carry

    def sources():
        lax.fori_loop(0, n, source_cols, 0)
        placed = spread_out(src_rows[...], cols_hot[:, pl.ds(0, n * shots)])
        for q in range(4):
            for r in range(4):
                pattern[q * 4 + r] = placed[
                    q * width : (q + 1) * width, r * length : (r + 1) * length
                ]

    def receivers(t):
        value = traces_v[t : t + 1, :]
        high = value.astype(BF16).astype(F32)
        hit = lax.broadcasted_iota(jnp.int32, (hot_cols, recvs), 0) == col_of(recv_cell)
        cols_hot[:, pl.ds(0, recvs)] = jnp.where(hit, high, 0.0).astype(BF16)
        cols_hot[:, pl.ds(recvs, recvs)] = jnp.where(hit, value - high, 0.0).astype(BF16)
        placed = spread_out(recv_rows[...], cols_hot[:, pl.ds(0, 2 * recvs)])
        for q in range(4):
            for r in range(4):
                inject[t, q * 4 + r] = placed[
                    q * width : (q + 1) * width, r * length : (r + 1) * length
                ]

    def laplace(field, z0, nz, x0, nx):
        column = field[pl.ds(z0, nz + 2 * HALO), pl.ds(pl.multiple_of(x0 + PAD, 8), nx), :]
        mid = column[HALO : HALO + nz]
        flat = mid.reshape(nz * nx, length)
        high = flat.astype(BF16)
        low = (flat - high.astype(F32)).astype(BF16)
        lanes = jnp.dot(
            jnp.concatenate([high, low], axis=1), band[...], preferred_element_type=F32
        ).reshape(nz, nx, length)
        total = CENTER * mid + lanes
        planes = pl.ds(z0 + HALO, nz)
        for k in range(4):
            near = column[HALO + 1 + k : HALO + 1 + k + nz] + column[3 - k : 3 - k + nz]
            near = near + field[planes, pl.ds(x0 + PAD + 1 + k, nx), :]
            near = near + field[planes, pl.ds(x0 + PAD - 1 - k, nx), :]
            total = total + RINGS[k] * near
        return mid, total

    faces = ((0, HALO), (depth - HALO, HALO))
    middle = ((HALO, depth - 2 * HALO),)

    def sweep(blocks, work, unroll=UNROLL):
        def tile(j, carry):
            x0 = pl.multiple_of(j * TILE, TILE)
            for z0, nz in blocks:
                work(z0, nz, x0)
            return carry

        lax.fori_loop(0, width // TILE, tile, 0, unroll=unroll)

    def face_sweep(work, h, field):
        for part_no in range(2):

            def tile(j, carry):
                x0 = pl.multiple_of(j * TILE + part_no * rows_half, TILE)
                for z0, nz in faces:
                    work(z0, nz, x0)
                return carry

            lax.fori_loop(0, rows_half // TILE, tile, 0, unroll=4)
            halo_stage(h, field, part_no)
            halo_start(h, field, part_no)

    def forward(t, now, prev, bare=False):
        def work(z0, nz, x0):
            planes = pl.ds(z0, nz)
            rows = pl.ds(x0, TILE)
            at = (pl.ds(z0 + HALO, nz), pl.ds(pl.multiple_of(x0 + PAD, 8), TILE))
            mid, image = laplace(now, z0, nz, x0, TILE)
            value = (mid + mid - prev[at]) + cour_v[planes, rows] * image
            if not bare:
                value = value + wavelet[t] * pattern[planes, rows]
            if t < steps - 1:
                prev[at] = value
            else:
                fwd_last[0, planes, rows] = value
            if t == 0:
                image_0[planes, rows] = image
            elif t == 1:
                image_1[planes, rows] = image
            elif t == 2:
                grad[planes, rows] = image * a_4[planes, rows]
            else:
                grad[planes, rows] += image * a_5[planes, rows]

        return work

    def add_pattern(z0, nz, x0):
        at = (pl.ds(z0 + HALO, nz), pl.ds(pl.multiple_of(x0 + PAD, 8), TILE))
        u_b[at] += wavelet[0] * pattern[pl.ds(z0, nz), pl.ds(x0, TILE)]

    def adjoint(t, w_now, w_next, now, later, new, bare=False):
        def work(z0, nz, x0):
            planes = pl.ds(z0, nz)
            rows = pl.ds(x0, TILE)
            _, along = laplace(w_now, z0, nz, x0, TILE)
            value = now[planes, rows]
            value = (value + value - later[planes, rows]) + along
            if not bare:
                value = value + inject[t, planes, rows]
                at = (pl.ds(z0 + HALO, nz), pl.ds(pl.multiple_of(x0 + PAD, 8), TILE))
                w_next[at] = cour_v[planes, rows] * value
            new[planes, rows] = value
            if t == 1:
                grad[planes, rows] += value * image_1[planes, rows]

        return work

    def add_inject(z0, nz, x0):
        planes = pl.ds(z0, nz)
        rows = pl.ds(x0, TILE)
        at = (pl.ds(z0 + HALO, nz), pl.ds(pl.multiple_of(x0 + PAD, 8), TILE))
        value = a_5[planes, rows] + inject[steps - 1, planes, rows]
        a_5[planes, rows] = value
        w_b[at] = cour_v[planes, rows] * value

    half = depth // 2
    side = math.isqrt(n)
    e_y, e_x = e // side, lax.rem(e, side)
    mine = ((e_y, e_x), (e_x, e_y))

    def owner(way, p, q):
        return p * side + q if way == 0 else q * side + p

    def first_copy(group, way, to, slot):
        return pltpu.make_async_remote_copy(
            src_ref=gsend.at[group, way, to],
            dst_ref=gfirst.at[group, way, slot],
            send_sem=first_send.at[group, way, to],
            recv_sem=first_recv.at[group, way, slot],
            device_id={"enc": owner(way, to, mine[way][1])},
            device_id_type=MESH,
        )

    def last_copy(group, way, to, slot):
        return pltpu.make_async_remote_copy(
            src_ref=gsum.at[group, way, to],
            dst_ref=glast.at[group, way, slot],
            send_sem=last_send.at[group, way, to],
            recv_sem=last_recv.at[group, way, slot],
            device_id={"enc": owner(way, mine[way][0], to)},
            device_id_type=MESH,
        )

    span = side * 8

    def last_adjoint(z0, nz, x0, nx):
        rows = pl.ds(x0, nx)
        planes = pl.ds(z0, nz)
        _, along = laplace(w_b, z0, nz, x0, nx)
        value = a_1[planes, rows]
        value = (value + value - a_4[planes, rows]) + along + inject[0, planes, rows]
        adj_first[0, planes, rows] = value
        return grad[planes, rows] + value * image_0[planes, rows]

    others = (2, 1, 3) if side == 4 else tuple(range(1, side))

    def last_step(group):
        for off in others + (0,):
            to = lax.rem(e_y + off, side)

            for at in range(0, span, TILE):
                x0 = pl.multiple_of(to * span + at, 8)
                if group == 0:
                    value = last_adjoint(HALO, half, x0, TILE)
                    lower, upper = value[:HALO], value[HALO:]
                else:
                    lower = last_adjoint(0, HALO, x0, TILE)
                    upper = last_adjoint(depth - HALO, HALO, x0, TILE)
                for r in range(TILE // 8):
                    gsend[group, 0, to, at // 8 + r] = lower[:, r * 8 : r * 8 + 8]
                    gsend[group, 1, at // 8 + r, to] = upper[:, r * 8 : r * 8 + 8]
            if off != 0:
                first_copy(group, 0, to, e_y).start()
        for off in others:
            first_copy(group, 1, lax.rem(e_x + off, side), e_x).start()

    def first_sum(group, way):
        p, q = mine[way]
        total = gsend[group, way, p]
        for off in range(1, side):
            slot = lax.rem(p + off, side)
            first_copy(group, way, slot, slot).wait_recv()
            total = total + gfirst[group, way, slot]
        gsum[group, way] = total
        for off in others:
            last_copy(group, way, lax.rem(q + off, side), q).start()

    def last_sum(group, way):
        q = mine[way][1]
        total = gsum[group, way, q]
        for off in range(1, side):
            slot = lax.rem(q + off, side)
            last_copy(group, way, slot, slot).wait_recv()
            total = total + glast[group, way, slot]
        z0 = HALO * (1 + way) if group == 0 else way * (depth - HALO)
        gradient[pl.ds(z0, HALO)] = total * (1.0 / (UNIT * steps * n))

    loads[4].wait()
    loads[5].wait()
    sweep(middle, forward(0, u_a, u_b, True))
    sweep(middle, adjoint(3, w_a, None, a_4, a_5, a_5, True))
    lax.fori_loop(1, n, sign_wait, 0)
    sources()
    halo_wait(0, u_a)
    face_sweep(forward(0, u_a, u_b), 2, u_b)
    lax.fori_loop(1, n, enc_wait, 0)
    total = parts[0, pl.ds(0, steps)]
    for i in range(1, n):
        total = total + parts[i, pl.ds(0, steps)]
    traces_v[...] = total * (1.0 / (shots * n) ** 0.5)
    receivers(3)
    halo_wait(1, w_a)
    face_sweep(adjoint(3, w_a, w_b, a_4, a_5, a_5), 3, w_b)
    sweep(middle, add_pattern)
    sweep(middle, add_inject)
    for t in range(3):
        receivers(2 - t)

    halo_sent(0, u_a)
    work = forward(1, u_b, u_a)
    halo_wait(2, u_b)
    face_sweep(work, 4, u_a)
    sweep(middle, work)

    halo_sent(1, w_a)
    work = adjoint(2, w_b, w_a, a_5, a_4, a_4)
    halo_wait(3, w_b)
    face_sweep(work, 5, w_a)
    sweep(middle, work)

    halo_sent(2, u_b)
    work = forward(2, u_a, u_b)
    halo_wait(4, u_a)
    face_sweep(work, 6, u_b)
    sweep(middle, work)

    halo_sent(3, w_b)
    work = adjoint(1, w_a, w_b, a_4, a_5, a_1)
    halo_wait(5, w_a)
    face_sweep(work, 7, w_b)
    sweep(middle, work)

    halo_sent(4, u_a)
    work = forward(3, u_b, u_a)
    sweep(middle, work)
    last_step(0)
    halo_wait(6, u_b)
    sweep(faces, work)

    halo_wait(7, w_b)
    last_step(1)
    for group in range(2):
        for way in range(2):
            first_sum(group, way)
    for group in range(2):
        for way in range(2):
            last_sum(group, way)

    def finish(k, carry):
        enc_copy(k, False).wait_send()
        sign_copy(k, False).wait_send()
        return carry

    lax.fori_loop(1, n, finish, 0)
    for group in range(2):
        for way in range(2):
            for off in others:
                to = lax.rem(mine[way][0] + off, side)
                first_copy(group, way, to, to).wait_send()
                to = lax.rem(mine[way][1] + off, side)
                last_copy(group, way, to, to).wait_send()
    halo_sent(5, w_a)
    halo_sent(6, u_b)
    halo_sent(7, w_b)


def store(share, fwd, adj, gradient, fwd_last, adj_first, sem):
    copies = [
        pltpu.make_async_copy(share, gradient, sem.at[0]),
        pltpu.make_async_copy(fwd, fwd_last, sem.at[1]),
        pltpu.make_async_copy(adj, adj_first, sem.at[2]),
    ]
    for copy in copies:
        copy.start()
    for copy in copies:
        copy.wait()


def body(
    n,
    nd,
    residual,
    weights,
    source_pos,
    receiver_pos,
    wavelet,
    courant,
    fwd_prev,
    fwd_now,
    adj_next,
    adj_now,
):
    shots, steps, recvs = residual.shape
    depth, width, length = courant.shape
    share = (depth, width // n, length)
    side = math.isqrt(n)
    field = pltpu.VMEM((depth, width, length), F32)
    padded = pltpu.VMEM((depth + 2 * HALO, width + 2 * PAD, length), F32)
    hot = max(2 * recvs, n * shots)
    anywhere = pl.BlockSpec(memory_space=pl.ANY)
    vmem = pl.BlockSpec(memory_space=pltpu.VMEM)
    results = pl.pallas_call(
        functools.partial(kernel, n, nd),
        out_shape=(
            pltpu.VMEM(share, F32),
            pltpu.VMEM((1, depth, width, length), F32),
            pltpu.VMEM((1, depth, width, length), F32),
        ),
        in_specs=[
            anywhere,
            vmem,
            vmem,
            vmem,
            pl.BlockSpec(memory_space=pltpu.SMEM),
            anywhere,
            anywhere,
            anywhere,
            anywhere,
            anywhere,
        ],
        out_specs=(vmem, vmem, vmem),
        scratch_shapes=[
            pltpu.VMEM((shots, steps, recvs), BF16),
            field,
            padded,
            padded,
            padded,
            padded,
            field,
            field,
            field,
            field,
            field,
            field,
            field,
            pltpu.VMEM((steps, depth, width, length), F32),
            pltpu.VMEM((2 * length, length), BF16),
            pltpu.VMEM((4 * width, n * shots), BF16),
            pltpu.VMEM((4 * width, 2 * recvs), BF16),
            pltpu.VMEM((4 * length, hot), BF16),
            pltpu.VMEM((n, 8, recvs), F32),
            pltpu.VMEM((n, 8, recvs), F32),
            pltpu.VMEM((steps, recvs), F32),
            pltpu.VMEM((n, 1, shots), F32),
            pltpu.VMEM((n, 1, shots), F32),
            pltpu.VMEM((2, 2, side, side, HALO) + share[1:], F32),
            pltpu.VMEM((2, 2, side, side, HALO) + share[1:], F32),
            pltpu.VMEM((2, 2, side, HALO) + share[1:], F32),
            pltpu.VMEM((2, 2, side, HALO) + share[1:], F32),
            pltpu.VMEM((8, 2, 2, HALO - 1, width // 2, length), BF16),
            pltpu.VMEM((8, 2, 2, HALO - 1, width // 2, length), BF16),
            pltpu.SemaphoreType.DMA((6,)),
            pltpu.SemaphoreType.DMA((n,)),
            pltpu.SemaphoreType.DMA((n,)),
            pltpu.SemaphoreType.DMA((n,)),
            pltpu.SemaphoreType.DMA((n,)),
            pltpu.SemaphoreType.DMA((8, 2, 2, 2)),
            pltpu.SemaphoreType.DMA((8, 2, 2, 2)),
            pltpu.SemaphoreType.DMA((2, 2, side)),
            pltpu.SemaphoreType.DMA((2, 2, side)),
            pltpu.SemaphoreType.DMA((2, 2, side)),
            pltpu.SemaphoreType.DMA((2, 2, side)),
        ],
        compiler_params=pltpu.CompilerParams(
            collective_id=0, has_side_effects=True, vmem_limit_bytes=58 * 2**20
        ),
    )(
        residual,
        weights,
        source_pos.reshape(n, 1, shots),
        receiver_pos.reshape(1, recvs),
        wavelet,
        courant,
        fwd_prev,
        fwd_now,
        adj_next,
        adj_now,
    )
    return pl.pallas_call(
        store,
        out_shape=tuple(jax.ShapeDtypeStruct(r.shape, F32) for r in results),
        in_specs=[vmem] * 3,
        out_specs=(anywhere,) * 3,
        scratch_shapes=[pltpu.SemaphoreType.DMA((3,))],
        compiler_params=pltpu.CompilerParams(vmem_limit_bytes=4 * 2**20),
    )(*results)


def solution(mesh):
    placed = (
        P("enc", None, "dom"),
        P(None, "enc"),
        P(),
        P("dom"),
        P(),
        P("dom", None, None),
        P("enc", "dom", None, None),
        P("enc", "dom", None, None),
        P("enc", "dom", None, None),
        P("enc", "dom", None, None),
    )
    return jax.shard_map(
        functools.partial(body, mesh.shape["enc"], mesh.shape["dom"]),
        mesh=mesh,
        in_specs=placed,
        out_specs=(P("dom", "enc", None), P("enc", "dom", None, None), P("enc", "dom", None, None)),
        check_vma=False,
    )
```
